32 devices in a mesh: group: 8 (over z, x), member: 4 (over y, core).
Axes of the slice: x: 2, y: 2, z: 4, core: 2. Of those that a mesh axis runs over, the one named last changes fastest.
Arguments:
- prompt_k: bfloat16 [8, 256, 1024], P('group', 'member'), may hold values from -6 to 6
- prompt_v: bfloat16 [8, 256, 1024], P('group', 'member'), may hold values from -18 to 18
- resp_q: bfloat16 [8, 4, 128, 4096], P('group', 'member'), may hold values from -45 to 45
- resp_k: bfloat16 [8, 4, 128, 1024], P('group', 'member'), may hold values from -6 to 6
- resp_v: bfloat16 [8, 4, 128, 1024], P('group', 'member'), may hold values from -18 to 18
- out_grad: bfloat16 [8, 4, 128, 4096], P('group', 'member'), may hold values from -6 to 6
- lengths: int32 [8, 4], P('group', 'member'), may hold values from 16 to 128, as said below
- rewards: float32 [8, 4], P('group', 'member'), may hold values from -6 to 6
Outputs:
- attended: bfloat16 [8, 4, 128, 4096], P('group', 'member')
- grad_q: bfloat16 [8, 4, 128, 4096], P('group', 'member')
- grad_resp_k: bfloat16 [8, 4, 128, 1024], P('group', 'member')
- grad_resp_v: bfloat16 [8, 4, 128, 1024], P('group', 'member')
- grad_prompt_k: bfloat16 [8, 256, 1024], P('group', 'member')
- grad_prompt_v: bfloat16 [8, 256, 1024], P('group', 'member')
The draws below stay inside these ranges and needn't reach their ends.
Inputs may be any that keep to these rules, and one draw needn't show every extreme that they name: In each group the lengths never fall from one member to the next, and the last member's response has exactly 128 live tokens.
All inputs are finite; a program needn't handle non-finite values.
Results may differ from the reference program's by a relative error of at most 0.0082.
Values may be sent and summed in bfloat16 or wider, within the bound.
A program may use at most 128 MiB of HBM per device.

```python
import jax
import jax.numpy as jnp
from jax import lax

H = 32
KVH = 8
HD = 128
CAP = 128
GROUPS = 8
RESP = 4
PROMPT = 256


def draw_prompt_k(key, part):
    key = jax.random.fold_in(key, 1)
    full_shape = (GROUPS, PROMPT, KVH * HD)
    return jnp.clip(jax.random.normal(key, full_shape, jnp.float32), -6.0, 6.0).astype(jnp.bfloat16)


def draw_resp_q(key, part):
    key = jax.random.fold_in(key, 2)
    full_shape = (GROUPS, RESP, CAP, H * HD)
    return jnp.clip(2.0 * jax.random.normal(key, full_shape, jnp.float32), -12.0, 12.0).astype(jnp.bfloat16)


def draw_lengths(key, part):
    key = jax.random.fold_in(key, 3)
    lowest = max(1, CAP // 8)
    drawn = jax.random.randint(key, (GROUPS, RESP), lowest, CAP + 1, jnp.int32)
    drawn = jnp.sort(drawn, axis=1)
    return drawn.at[:, RESP - 1].set(CAP)


def block_scale(key, dims, cuts, least, largest):
    factor_of, own = 1.0, jax.random.fold_in(key, 6)
    for dim, parts in cuts:
        heights = jnp.exp(jax.random.uniform(jax.random.fold_in(own, dim), (parts,), jnp.float32, least / len(cuts), largest / len(cuts)))
        factor_of = factor_of * jnp.repeat(heights, dims[dim] // parts).reshape([-1 if axis == dim else 1 for axis in range(len(dims))])
    return factor_of


def scatter_about(key, shape, spread, limit, cuts=(), held_as=jnp.bfloat16):
    factor_of = block_scale(key, shape, cuts, -0.22, 0.18) if cuts else 1.0
    result = jax.random.normal(key, shape, jnp.float32) * spread * factor_of
    return jnp.minimum(jnp.maximum(result, -limit), limit).astype(held_as)


def setup_inputs(seed: int = 0) -> dict:
    keys = jax.random.split(jax.random.key(seed), 9)
    prompt_k = draw_prompt_k(jax.random.fold_in(keys[8], 71), 0)
    prompt_v = scatter_about(keys[1], (GROUPS, PROMPT, KVH * HD), 3.0, 18.0, ((0, 8), (1, 4)))
    resp_q = draw_resp_q(jax.random.fold_in(keys[8], 71), 0)
    resp_k = scatter_about(keys[3], (GROUPS, RESP, CAP, KVH * HD), 1.0, 6.0, ((0, 8), (1, 4)))
    resp_v = scatter_about(keys[4], (GROUPS, RESP, CAP, KVH * HD), 3.0, 18.0, ((0, 8), (1, 4)))
    out_grad = scatter_about(keys[5], (GROUPS, RESP, CAP, H * HD), 1.0, 6.0, ((0, 8), (1, 4)))
    lengths = draw_lengths(jax.random.fold_in(keys[8], 71), 0)
    rewards = scatter_about(keys[7], (GROUPS, RESP), 1.0, 6.0, ((0, 8), (1, 4)), jnp.float32)
    return dict(prompt_k=prompt_k, prompt_v=prompt_v, resp_q=resp_q, resp_k=resp_k, resp_v=resp_v, out_grad=out_grad, lengths=lengths, rewards=rewards)


def to_heads(rows_in, kv_heads, head_size):
    row_count = rows_in.shape[0]
    per_head = rows_in.shape[1] // (kv_heads * head_size)
    shaped = rows_in.reshape(row_count, kv_heads, per_head, head_size)
    return shaped.transpose(1, 2, 0, 3).reshape(kv_heads, per_head * row_count, head_size)


def from_heads(blocks, row_count):
    kv_heads, rows_all, head_size = blocks.shape
    per_head = rows_all // row_count
    shaped = blocks.reshape(kv_heads, per_head, row_count, head_size)
    return shaped.transpose(2, 0, 1, 3).reshape(row_count, kv_heads * per_head * head_size)


def head_terms(queries, cotangent, all_keys, all_values, allowed, first_key, score_scale):
    scores = jnp.dot(queries, all_keys.T, preferred_element_type=jnp.float32) * score_scale
    scores = jnp.where(allowed, scores, -jnp.inf)
    row_max = jnp.max(scores, axis=1, keepdims=True)
    raised = jnp.exp(scores - row_max)
    row_sum = jnp.sum(raised, axis=1, keepdims=True)
    probability = raised / row_sum
    probs_low = probability.astype(jnp.bfloat16)
    output = jnp.dot(probs_low, all_values, preferred_element_type=jnp.float32)
    dprobs = jnp.dot(cotangent, all_values.T, preferred_element_type=jnp.float32)
    row_delta = jnp.sum(cotangent.astype(jnp.float32) * output, axis=1, keepdims=True)
    dscores = (probability * (dprobs - row_delta)).astype(jnp.bfloat16)
    grad_query = jnp.dot(dscores, all_keys, preferred_element_type=jnp.float32) * score_scale
    grad_keys = jnp.dot(dscores[:, first_key:].T, queries, preferred_element_type=jnp.float32) * score_scale
    grad_values = jnp.dot(probs_low[:, first_key:].T, cotangent, preferred_element_type=jnp.float32)
    return output, grad_query, grad_keys, grad_values, row_max, row_sum, row_delta


def reference(prompt_k, prompt_v, resp_q, resp_k, resp_v, out_grad, lengths, rewards):
    score_scale = float(HD) ** -0.5
    token_total = jnp.sum(lengths.astype(jnp.float32))
    factor = jnp.float32(CAP * GROUPS * RESP) / token_total
    advantage = rewards - jnp.sum(rewards, axis=1, keepdims=True) / RESP
    position = jnp.arange(CAP)
    per_head = H // KVH
    row_pos = jnp.tile(position, per_head)
    key_pos = jnp.arange(PROMPT + CAP)
    allowed = (key_pos[None, :] < PROMPT) | (key_pos[None, :] - PROMPT <= row_pos[:, None])

    def one_group(group_inputs):
        group_k, group_v, queries_all, rkeys_all, rvalues_all, upstream_all, length_all, advantage_all = group_inputs

        def one_response(carry, inputs):
            queries, rkeys, rvalues, upstream, length, adv_one = inputs
            live_rows = position < length
            weight = jnp.where(live_rows, adv_one * factor, 0.0).astype(jnp.float32)
            cotangent = (upstream.astype(jnp.float32) * weight[:, None]).astype(jnp.bfloat16)
            all_keys = jnp.concatenate([group_k, rkeys], axis=0)
            all_values = jnp.concatenate([group_v, rvalues], axis=0)
            operands = (to_heads(queries, KVH, HD), to_heads(cotangent, KVH, HD),
                        to_heads(all_keys, KVH, HD), to_heads(all_values, KVH, HD))

            def per_kv_head(head_ops):
                return head_terms(head_ops[0], head_ops[1], head_ops[2], head_ops[3], allowed, 0, score_scale)

            output, grad_query, grad_keys, grad_values, row_max, row_sum, row_delta = lax.map(per_kv_head, operands)
            attended = (from_heads(output, CAP) * live_rows[:, None]).astype(jnp.bfloat16)
            grad_q = from_heads(grad_query, CAP).astype(jnp.bfloat16)
            key_rows = from_heads(grad_keys, PROMPT + CAP)
            value_rows = from_heads(grad_values, PROMPT + CAP)
            carry = (carry[0] + key_rows[:PROMPT], carry[1] + value_rows[:PROMPT])
            return carry, (attended, grad_q, key_rows[PROMPT:].astype(jnp.bfloat16), value_rows[PROMPT:].astype(jnp.bfloat16))

        zeros_init = jnp.zeros((PROMPT, KVH * HD), jnp.float32)
        sums, outputs = lax.scan(one_response, (zeros_init, zeros_init),
                                 (queries_all, rkeys_all, rvalues_all, upstream_all, length_all, advantage_all))
        return outputs + (sums[0].astype(jnp.bfloat16), sums[1].astype(jnp.bfloat16))

    results = lax.map(one_group, (prompt_k, prompt_v, resp_q, resp_k, resp_v, out_grad, lengths, advantage))
    return results[0], results[1], results[2], results[3], results[4], results[5]
```

```python
import functools

import jax
import jax.numpy as jnp
from jax import lax
from jax.experimental import pallas as pl
from jax.experimental.pallas import tpu as pltpu
from jax.sharding import PartitionSpec as P

KVH = 8
HD = 128
LOG2E = 1.4426950408889634
MESH = pl.DeviceIdType.MESH
NT = (((1,), (1,)), ((), ()))
NN = (((1,), (0,)), ((), ()))
TN = (((0,), (0,)), ((), ()))


def dot(a, b, dims):
    return lax.dot_general(a, b, dims, preferred_element_type=jnp.float32)


def kernel(
    groups, members, rows, slots, per_head,
    length_ref, reward_ref, pk_ref, pv_ref, q_ref, rk_ref, rv_ref, og_ref,
    att_out, gq_out, grk_out, grv_out, gpk_out, gpv_out,
    kall, vall, qbuf, obuf, att, gq, grk, grv, gpk, gpv,
    part, sib_send, sib_recv, x_send, x_recv, stat_send, stat, tok_send, tok, fac,
    in_sem, g_send, f_send, g_recv, s_send, s_recv, t_send, t_recv,
    r_send, r_recv, c_send, c_recv, out_sem, end_sem,
):
    chips = members // 2
    prompt = members * rows
    wide = per_head * slots
    score_scale = float(HD) ** (-0.5)
    group = lax.axis_index("group")
    me = lax.axis_index("member")
    chip = lax.div(me, 2)
    core = lax.rem(me, 2)
    sib = chip * 2 + (1 - core)

    def chip_at(d):
        return lax.rem(chip + d, chips)

    def cols(j, width=HD):
        return pl.ds(pl.multiple_of(j * width, width), width)

    def block_rows(owner):
        return pl.ds(pl.multiple_of(owner * rows, rows), rows)

    def local(src, dst, sem):
        return pltpu.make_async_copy(src, dst, sem)

    def remote(src, dst, send, recv, to_group, to_member):
        return pltpu.make_async_remote_copy(
            src_ref=src, dst_ref=dst, send_sem=send, recv_sem=recv,
            device_id=(to_group, to_member), device_id_type=MESH)

    loads = [
        local(pk_ref.at[0], kall.at[block_rows(me)], in_sem.at[0]),
        local(pv_ref.at[0], vall.at[block_rows(me)], in_sem.at[1]),
        local(rk_ref.at[0, 0], kall.at[pl.ds(prompt, slots)], in_sem.at[2]),
        local(rv_ref.at[0, 0], vall.at[pl.ds(prompt, slots)], in_sem.at[3]),
        local(q_ref.at[0, 0], qbuf, in_sem.at[4]),
        local(og_ref.at[0, 0], obuf, in_sem.at[5]),
    ]
    for load in loads:
        load.start()

    barrier = pltpu.get_barrier_semaphore()
    for step in range(1, members):
        pl.semaphore_signal(barrier, inc=1, device_id=(group, lax.rem(me + step, members)), device_id_type=MESH)
    for step in range(1, groups):
        pl.semaphore_signal(barrier, inc=1, device_id=(lax.rem(group + step, groups), me), device_id_type=MESH)

    length = length_ref[0, 0]
    stat_send[0] = jnp.full((8, HD), length.astype(jnp.float32))
    stat_send[1] = jnp.full((8, HD), reward_ref[0, 0])
    stat[me] = stat_send[...]
    pl.semaphore_wait(barrier, members - 1 + groups - 1)

    sides = ((pk_ref, kall), (pv_ref, vall))

    def direct(side, j, slot):
        to = sib if slot == 0 else chip_at(slot) * 2 + core
        source, whole = sides[side]
        return remote(source.at[0, :, cols(j)], whole.at[block_rows(me), cols(j)],
                      g_send.at[side, j, slot], g_recv.at[side, j, me], group, to)

    def arrival(side, j, owner):
        place = sides[side][1].at[block_rows(owner), cols(j)]
        return remote(place, place, g_send.at[side, j, 0], g_recv.at[side, j, owner], group, sib)

    def forward(side, j, d):
        owner = chip_at(d) * 2 + core
        place = sides[side][1].at[block_rows(owner), cols(j)]
        return remote(place, place, f_send.at[side, j, d - 1], g_recv.at[side, j, owner], group, sib)

    def stat_copy(step):
        return remote(stat_send, stat.at[me], s_send.at[step - 1], s_recv.at[me], group, lax.rem(me + step, members))

    def tok_copy(step):
        return remote(tok_send, tok.at[group], t_send.at[step - 1], t_recv.at[group],
                      lax.rem(group + step, groups), me)

    def send_head(j, carry):
        for slot in list(range(1, chips)) + [0]:
            for side in range(2):
                direct(side, j, slot).start()
        return carry

    send_head(0, 0)
    for step in range(1, members):
        stat_copy(step).start()
    lax.fori_loop(1, KVH, send_head, 0)

    for step in range(1, members):
        owner = lax.rem(me + step, members)
        remote(stat_send, stat.at[owner], s_send.at[0], s_recv.at[owner], group, owner).wait_recv()
    tok_send[...] = functools.reduce(jnp.add, [stat[i, 0] for i in range(members)])
    tok[group] = tok_send[...]
    for step in range(1, groups):
        tok_copy(step).start()
    reward_total = functools.reduce(jnp.add, [stat[i, 1] for i in range(members)])
    advantage = stat_send[1] - reward_total / members
    adv_row = advantage[0:1]

    def forward_head(j):
        for d in range(1, chips):
            owner = chip_at(d) * 2 + core
            for side in range(2):
                arrival(side, j, owner).wait_recv()
                forward(side, j, d).start()

    forward_head(0)
    for load in loads:
        load.wait()

    u_pos = lax.broadcasted_iota(jnp.int32, (slots, wide), 0)
    t_pos = lax.rem(lax.broadcasted_iota(jnp.int32, (slots, wide), 1), slots)
    causal = u_pos <= t_pos
    live_lane = lax.rem(lax.broadcasted_iota(jnp.int32, (HD, wide), 1), slots) < length
    live_row = lax.rem(lax.broadcasted_iota(jnp.int32, (wide, HD), 0), slots) < length

    def sib_copy(j):
        return remote(sib_send.at[j], sib_recv.at[j], r_send.at[j], r_recv.at[j], group, sib)

    def cross_copy(j, d):
        return remote(x_send.at[j, d - 1], x_recv.at[j, d - 1], c_send.at[j, d - 1], c_recv.at[j, d - 1],
                      group, chip_at(d) * 2 + core)

    def cross_head(j):
        sib_copy(j).wait_recv()
        for d in range(1, chips):
            own = part[j, chip_at(d) * 2 + core]
            x_send[j, d - 1] = (own + sib_recv[j, d].astype(jnp.float32)).astype(jnp.bfloat16)
            cross_copy(j, d).start()

    def out_copies(j):
        return [
            local(att.at[:, cols(j, per_head * HD)], att_out.at[0, 0, :, cols(j, per_head * HD)], out_sem.at[0, j]),
            local(gq.at[:, cols(j, per_head * HD)], gq_out.at[0, 0, :, cols(j, per_head * HD)], out_sem.at[1, j]),
            local(grk.at[:, cols(j)], grk_out.at[0, 0, :, cols(j)], out_sem.at[2, j]),
            local(grv.at[:, cols(j)], grv_out.at[0, 0, :, cols(j)], out_sem.at[3, j]),
        ]

    def head(j, carry):
        @pl.when(j + 1 < KVH)
        def _():
            forward_head(j + 1)

        for side in range(2):
            arrival(side, j, sib).wait_recv()
            for d in range(1, chips):
                arrival(side, j, chip_at(d) * 2 + (1 - core)).wait_recv()

        k = kall[:, cols(j)]
        v = vall[:, cols(j)]
        qs = [qbuf[:, cols(j * per_head + h)] for h in range(per_head)]
        gs = [obuf[:, cols(j * per_head + h)] for h in range(per_head)]
        q = jnp.concatenate(qs, axis=0)
        g = jnp.concatenate(gs, axis=0)
        g = jnp.where(live_row, g, jnp.zeros_like(g))
        s = dot(k, q, NT)
        s = jnp.concatenate([s[:prompt], jnp.where(causal, s[prompt:], -1e30)], axis=0)
        top = jnp.max(s, axis=0, keepdims=True)
        e = jnp.exp2((s - top) * (score_scale * LOG2E))
        p = e * (1.0 / jnp.sum(e, axis=0, keepdims=True))
        p_low = p.astype(jnp.bfloat16)
        dp = dot(v, g, NT)
        delta = jnp.sum(p * dp, axis=0, keepdims=True)
        ds = (p * (dp - delta)).astype(jnp.bfloat16)
        dk = dot(ds, q, NN) * (adv_row * score_scale)
        dv = dot(p_low, g, NN) * adv_row
        part[j, :, :, :HD] = dk[:prompt].reshape(members, rows, HD)
        part[j, :, :, HD:] = dv[:prompt].reshape(members, rows, HD)
        for d in range(chips):
            sib_send[j, d] = part[j, chip_at(d) * 2 + (1 - core)].astype(jnp.bfloat16)
        sib_copy(j).start()

        @pl.when(j == 0)
        def _():
            for step in range(1, groups):
                owner = lax.rem(group + step, groups)
                remote(tok_send, tok.at[owner], t_send.at[0], t_recv.at[owner], owner, me).wait_recv()
            total = functools.reduce(jnp.add, [tok[i] for i in range(groups)])
            fac[...] = float(slots * groups * members) / total

        factor = fac[0:1]
        grk[:, cols(j)] = (dk[prompt:] * factor).astype(jnp.bfloat16)
        grv[:, cols(j)] = (dv[prompt:] * factor).astype(jnp.bfloat16)
        o_t = dot(v, p_low, TN)
        o_t = jnp.where(live_lane, o_t, 0.0).astype(jnp.bfloat16)
        dq_t = dot(k, ds, TN)
        weight = (adv_row * factor) * score_scale
        dq_t = (dq_t * weight[0:1, 0:1]).astype(jnp.bfloat16)
        for h in range(per_head):
            att[:, cols(j * per_head + h)] = o_t[:, h * slots:(h + 1) * slots].T
            gq[:, cols(j * per_head + h)] = dq_t[:, h * slots:(h + 1) * slots].T
        for copy in out_copies(j):
            copy.start()

        @pl.when(j > 0)
        def _():
            cross_head(j - 1)

        return carry

    lax.fori_loop(0, KVH, head, 0)
    cross_head(KVH - 1)

    def finish(j, carry):
        total = part[j, me] + sib_recv[j, 0].astype(jnp.float32)
        for d in range(1, chips):
            cross_copy(j, d).wait_recv()
            total = total + x_recv[j, d - 1].astype(jnp.float32)
        factor = fac[0:1]
        gpk[:, cols(j)] = (total[:, :HD] * factor).astype(jnp.bfloat16)
        gpv[:, cols(j)] = (total[:, HD:] * factor).astype(jnp.bfloat16)
        return carry

    lax.fori_loop(0, KVH, finish, 0)
    ends = [local(gpk, gpk_out.at[0], end_sem.at[0]), local(gpv, gpv_out.at[0], end_sem.at[1])]
    for copy in ends:
        copy.start()

    def drain(j, carry):
        for side in range(2):
            for slot in range(chips):
                direct(side, j, slot).wait_send()
            for d in range(1, chips):
                forward(side, j, d).wait_send()
        sib_copy(j).wait_send()
        for d in range(1, chips):
            cross_copy(j, d).wait_send()
        for copy in out_copies(j):
            copy.wait()
        return carry

    lax.fori_loop(0, KVH, drain, 0)
    for step in range(1, members):
        stat_copy(step).wait_send()
    for step in range(1, groups):
        tok_copy(step).wait_send()
    for copy in ends:
        copy.wait()


def body(prompt_k, prompt_v, resp_q, resp_k, resp_v, out_grad, lengths, rewards):
    members = lax.axis_size("member")
    groups = lax.axis_size("group")
    chips = members // 2
    rows = prompt_k.shape[1]
    slots = resp_q.shape[2]
    per_head = resp_q.shape[3] // (KVH * HD)
    keys = members * rows + slots
    width = KVH * HD
    bf, f32 = jnp.bfloat16, jnp.float32
    dma = pltpu.SemaphoreType.DMA
    crossing = max(chips - 1, 1)
    scratch = [
        pltpu.VMEM((keys, width), bf),
        pltpu.VMEM((keys, width), bf),
        pltpu.VMEM((slots, width * per_head), bf),
        pltpu.VMEM((slots, width * per_head), bf),
        pltpu.VMEM((slots, width * per_head), bf),
        pltpu.VMEM((slots, width * per_head), bf),
        pltpu.VMEM((slots, width), bf),
        pltpu.VMEM((slots, width), bf),
        pltpu.VMEM((rows, width), bf),
        pltpu.VMEM((rows, width), bf),
        pltpu.VMEM((KVH, members, rows, 2 * HD), f32),
        pltpu.VMEM((KVH, chips, rows, 2 * HD), bf),
        pltpu.VMEM((KVH, chips, rows, 2 * HD), bf),
        pltpu.VMEM((KVH, crossing, rows, 2 * HD), bf),
        pltpu.VMEM((KVH, crossing, rows, 2 * HD), bf),
        pltpu.VMEM((2, 8, HD), f32),
        pltpu.VMEM((members, 2, 8, HD), f32),
        pltpu.VMEM((8, HD), f32),
        pltpu.VMEM((groups, 8, HD), f32),
        pltpu.VMEM((8, HD), f32),
        dma((6,)),
        dma((2, KVH, chips)),
        dma((2, KVH, crossing)),
        dma((2, KVH, members)),
        dma((members,)),
        dma((members,)),
        dma((groups,)),
        dma((groups,)),
        dma((KVH,)),
        dma((KVH,)),
        dma((KVH, crossing)),
        dma((KVH, crossing)),
        dma((4, KVH)),
        dma((2,)),
    ]
    held = pl.BlockSpec(memory_space=pl.ANY)
    scalar = pl.BlockSpec(memory_space=pltpu.SMEM)
    flops = 10 * slots * width * per_head * keys
    moved = sum(2 * a.size * a.dtype.itemsize for a in (resp_q, out_grad, resp_k, resp_v, prompt_k, prompt_v))
    return pl.pallas_call(
        functools.partial(kernel, groups, members, rows, slots, per_head),
        out_shape=[
            jax.ShapeDtypeStruct(a.shape, bf) for a in (resp_q, resp_q, resp_k, resp_v, prompt_k, prompt_v)
        ],
        in_specs=[scalar, scalar] + [held] * 6,
        out_specs=[held] * 6,
        scratch_shapes=scratch,
        compiler_params=pltpu.CompilerParams(
            collective_id=0, has_side_effects=True, vmem_limit_bytes=48 * 1024 * 1024),
        cost_estimate=pl.CostEstimate(
            flops=flops, bytes_accessed=moved, transcendentals=slots * KVH * per_head * keys),
        name="shared_prompt_attention",
    )(lengths, rewards, prompt_k, prompt_v, resp_q, resp_k, resp_v, out_grad)


def solution(mesh):
    rows = P("group", "member", None)
    wide = P("group", "member", None, None)
    return jax.shard_map(
        body,
        mesh=mesh,
        in_specs=(rows, rows, wide, wide, wide, wide, P("group", "member"), P("group", "member")),
        out_specs=(wide, wide, wide, wide, rows, rows),
        check_vma=False,
    )
```

```python
import functools

import jax
import jax.numpy as jnp
from jax import lax
from jax.experimental import pallas as pl
from jax.experimental.pallas import tpu as pltpu
from jax.sharding import PartitionSpec as P

KVH = 8
HD = 128
LOG2E = 1.4426950408889634
MESH = pl.DeviceIdType.MESH
NT = (((1,), (1,)), ((), ()))
NN = (((1,), (0,)), ((), ()))
TN = (((0,), (0,)), ((), ()))


def dot(a, b, dims):
    return lax.dot_general(a, b, dims, preferred_element_type=jnp.float32)


def kernel(
    groups, members, rows, slots, per_head,
    length_ref, reward_ref, pk_ref, pv_ref, q_ref, rk_ref, rv_ref, og_ref,
    att_out, gq_out, grk_out, grv_out, gpk_out, gpv_out,
    kall, vall, qbuf, obuf, att, gq, grk, grv, grk_low, grv_low, gpk, gpv,
    probs0, probs1, dsc0, dsc1,
    part, sib_send, sib_recv, x_send, x_recv, stat_send, stat, tok_send, tok,
    in_sem, g_send, f_send, g_recv, s_send, s_recv, t_send, t_recv,
    r_send, r_recv, c_send, c_recv, out_sem, end_sem,
):
    chips = members // 2
    prompt = members * rows
    wide = per_head * slots
    score_scale = float(HD) ** (-0.5)
    group = lax.axis_index("group")
    me = lax.axis_index("member")
    chip = lax.div(me, 2)
    core = lax.rem(me, 2)
    sib = chip * 2 + (1 - core)

    def chip_at(d):
        return lax.rem(chip + d, chips)

    def cols(j, width=HD):
        return pl.ds(pl.multiple_of(j * width, width), width)

    def block_rows(owner):
        return pl.ds(pl.multiple_of(owner * rows, rows), rows)

    def local(src, dst, sem):
        return pltpu.make_async_copy(src, dst, sem)

    def remote(src, dst, send, recv, to_group, to_member):
        return pltpu.make_async_remote_copy(
            src_ref=src, dst_ref=dst, send_sem=send, recv_sem=recv,
            device_id=(to_group, to_member), device_id_type=MESH)

    loads = [
        local(pk_ref.at[0], kall.at[block_rows(me)], in_sem.at[0]),
        local(pv_ref.at[0], vall.at[block_rows(me)], in_sem.at[1]),
        local(rk_ref.at[0, 0], kall.at[pl.ds(prompt, slots)], in_sem.at[2]),
        local(rv_ref.at[0, 0], vall.at[pl.ds(prompt, slots)], in_sem.at[3]),
        local(q_ref.at[0, 0], qbuf, in_sem.at[4]),
        local(og_ref.at[0, 0], obuf, in_sem.at[5]),
    ]
    for load in loads:
        load.start()

    barrier = pltpu.get_barrier_semaphore()
    for step in range(1, members):
        pl.semaphore_signal(barrier, inc=1, device_id=(group, lax.rem(me + step, members)), device_id_type=MESH)
    for step in range(1, groups):
        pl.semaphore_signal(barrier, inc=1, device_id=(lax.rem(group + step, groups), me), device_id_type=MESH)

    length = length_ref[0, 0]
    stat_send[0] = jnp.full((8, HD), length.astype(jnp.float32))
    stat_send[1] = jnp.full((8, HD), reward_ref[0, 0])
    stat[me] = stat_send[...]
    pl.semaphore_wait(barrier, members - 1 + groups - 1)

    sides = ((pk_ref, kall), (pv_ref, vall))

    def direct(side, j, slot):
        to = sib if slot == 0 else chip_at(slot) * 2 + core
        source, whole = sides[side]
        return remote(source.at[0, :, cols(j)], whole.at[block_rows(me), cols(j)],
                      g_send.at[side, j, slot], g_recv.at[side, j, me], group, to)

    def arrival(side, j, owner):
        place = sides[side][1].at[block_rows(owner), cols(j)]
        return remote(place, place, g_send.at[side, j, 0], g_recv.at[side, j, owner], group, sib)

    def forward(side, j, d):
        owner = chip_at(d) * 2 + core
        place = sides[side][1].at[block_rows(owner), cols(j)]
        return remote(place, place, f_send.at[side, j, d - 1], g_recv.at[side, j, owner], group, sib)

    def stat_copy(step):
        return remote(stat_send, stat.at[me], s_send.at[step - 1], s_recv.at[me], group, lax.rem(me + step, members))

    def tok_copy(step):
        return remote(tok_send, tok.at[group], t_send.at[step - 1], t_recv.at[group],
                      lax.rem(group + step, groups), me)

    def send_head(j, carry):
        for slot in list(range(1, chips)) + [0]:
            for side in range(2):
                direct(side, j, slot).start()
        return carry

    send_head(0, 0)
    for step in range(1, members):
        stat_copy(step).start()
    lax.fori_loop(1, KVH, send_head, 0)

    def forward_head(j):
        for d in range(1, chips):
            owner = chip_at(d) * 2 + core
            for side in range(2):
                arrival(side, j, owner).wait_recv()
                forward(side, j, d).start()

    def wait_head(j):
        for side in range(2):
            arrival(side, j, sib).wait_recv()
            for d in range(1, chips):
                arrival(side, j, chip_at(d) * 2 + (1 - core)).wait_recv()

    u_pos = lax.broadcasted_iota(jnp.int32, (slots, wide), 0)
    t_pos = lax.rem(lax.broadcasted_iota(jnp.int32, (slots, wide), 1), slots)
    causal = u_pos <= t_pos
    live_lane = lax.rem(lax.broadcasted_iota(jnp.int32, (HD, wide), 1), slots) < length
    live_row = lax.broadcasted_iota(jnp.int32, (slots, per_head * HD), 0) < length

    for load in loads:
        load.wait()

    def mask_head(j, carry):
        g = obuf[:, cols(j, per_head * HD)]
        obuf[:, cols(j, per_head * HD)] = jnp.where(live_row, g, jnp.zeros_like(g))
        return carry

    lax.fori_loop(0, KVH, mask_head, 0)

    forward_head(0)
    for step in range(1, members):
        owner = lax.rem(me + step, members)
        remote(stat_send, stat.at[owner], s_send.at[0], s_recv.at[owner], group, owner).wait_recv()
    tok_send[...] = functools.reduce(jnp.add, [stat[i, 0] for i in range(members)])
    tok[group] = tok_send[...]
    for step in range(1, groups):
        tok_copy(step).start()
    reward_total = functools.reduce(jnp.add, [stat[i, 1] for i in range(members)])
    advantage = stat_send[1] - reward_total / members
    adv_row = advantage[0:1]
    adv_one = adv_row[:, 0:1]
    forward_head(1)

    def sib_copy(j):
        return remote(sib_send.at[j], sib_recv.at[j], r_send.at[j], r_recv.at[j], group, sib)

    def cross_copy(j, d):
        return remote(x_send.at[j, d - 1], x_recv.at[j, d - 1], c_send.at[j, d - 1], c_recv.at[j, d - 1],
                      group, chip_at(d) * 2 + core)

    def cross_head(j):
        sib_copy(j).wait_recv()
        for d in range(1, chips):
            own = part[j, chip_at(d) * 2 + core]
            x_send[j, d - 1] = (own + sib_recv[j, d].astype(jnp.float32)).astype(jnp.bfloat16)
            cross_copy(j, d).start()

    def out_copy(kind, j):
        held, out, width = ((att, att_out, per_head * HD), (gq, gq_out, per_head * HD),
                            (grk_low, grk_out, HD), (grv_low, grv_out, HD))[kind]
        return local(held.at[:, cols(j, width)], out.at[0, 0, :, cols(j, width)], out_sem.at[kind, j])

    def stacked(buf, j):
        return jnp.concatenate([buf[:, cols(j * per_head + h)] for h in range(per_head)], axis=0)

    def heads(back, fore, back_bufs, fore_bufs):
        if fore is not None:
            s = dot(kall[:, cols(fore)], stacked(qbuf, fore), NT)
        if back is not None:
            p_back = back_bufs[0][...]
            dv = dot(p_back, stacked(obuf, back), NN) * adv_row
            o_t = dot(vall[:, cols(back)], p_back, TN)
        if fore is not None:
            s = jnp.concatenate([s[:prompt], jnp.where(causal, s[prompt:], -1e30)], axis=0)
            top = jnp.max(s, axis=0, keepdims=True)
            e = jnp.exp2((s - top) * (score_scale * LOG2E))
            p = e * (1.0 / jnp.sum(e, axis=0, keepdims=True))
            fore_bufs[0][...] = p.astype(jnp.bfloat16)
            dp = dot(vall[:, cols(fore)], stacked(obuf, fore), NT)
        if back is not None:
            ds_back = back_bufs[1][...]
            dk = dot(ds_back, stacked(qbuf, back), NN) * (adv_row * score_scale)
            dq_t = dot(kall[:, cols(back)], ds_back, TN) * (adv_one * score_scale)
        if fore is not None:
            delta = jnp.sum(p * dp, axis=0, keepdims=True)
            fore_bufs[1][...] = (p * (dp - delta)).astype(jnp.bfloat16)
        if back is not None:
            part[back, :, :, :HD] = dk[:prompt].reshape(members, rows, HD)
            part[back, :, :, HD:] = dv[:prompt].reshape(members, rows, HD)
            grk[:, cols(back)] = dk[prompt:]
            grv[:, cols(back)] = dv[prompt:]
            o_t = jnp.where(live_lane, o_t, 0.0).astype(jnp.bfloat16)
            dq_t = dq_t.astype(jnp.bfloat16)
            for h in range(per_head):
                att[:, cols(back * per_head + h)] = o_t[:, h * slots:(h + 1) * slots].T
                gq[:, cols(back * per_head + h)] = dq_t[:, h * slots:(h + 1) * slots].T
            for d in range(chips):
                sib_send[back, d] = part[back, chip_at(d) * 2 + (1 - core)].astype(jnp.bfloat16)
            sib_copy(back).start()
            out_copy(0, back).start()

    bufs = ((probs0, dsc0), (probs1, dsc1))
    wait_head(0)
    heads(None, 0, None, bufs[0])

    def pair(i, carry):
        j = 2 * i
        forward_head(j + 2)
        wait_head(j + 1)
        heads(j, j + 1, bufs[0], bufs[1])

        @pl.when(i > 0)
        def _():
            cross_head(j - 1)

        forward_head(j + 3)
        wait_head(j + 2)
        heads(j + 1, j + 2, bufs[1], bufs[0])
        cross_head(j)
        return carry

    lax.fori_loop(0, KVH // 2 - 1, pair, 0)
    wait_head(KVH - 1)
    heads(KVH - 2, KVH - 1, bufs[0], bufs[1])
    cross_head(KVH - 3)
    heads(KVH - 1, None, bufs[1], None)
    cross_head(KVH - 2)
    cross_head(KVH - 1)

    for step in range(1, groups):
        owner = lax.rem(group + step, groups)
        remote(tok_send, tok.at[owner], t_send.at[0], t_recv.at[owner], owner, me).wait_recv()
    tokens = functools.reduce(jnp.add, [tok[i] for i in range(groups)])
    factor = (float(slots * groups * members) / tokens)[0:1]
    factor_one = factor[:, 0:1]

    def scale_head(j, carry):
        span = cols(j, per_head * HD)
        gq[:, span] = (gq[:, span].astype(jnp.float32) * factor_one).astype(jnp.bfloat16)
        grk_low[:, cols(j)] = (grk[:, cols(j)] * factor).astype(jnp.bfloat16)
        grv_low[:, cols(j)] = (grv[:, cols(j)] * factor).astype(jnp.bfloat16)
        for kind in range(1, 4):
            out_copy(kind, j).start()
        return carry

    lax.fori_loop(0, KVH, scale_head, 0)

    def finish(j, carry):
        total = part[j, me] + sib_recv[j, 0].astype(jnp.float32)
        for d in range(1, chips):
            cross_copy(j, d).wait_recv()
            total = total + x_recv[j, d - 1].astype(jnp.float32)
        gpk[:, cols(j)] = (total[:, :HD] * factor).astype(jnp.bfloat16)
        gpv[:, cols(j)] = (total[:, HD:] * factor).astype(jnp.bfloat16)
        return carry

    lax.fori_loop(0, KVH, finish, 0)
    ends = [local(gpk, gpk_out.at[0], end_sem.at[0]), local(gpv, gpv_out.at[0], end_sem.at[1])]
    for copy in ends:
        copy.start()

    def drain(j, carry):
        for side in range(2):
            for slot in range(chips):
                direct(side, j, slot).wait_send()
            for d in range(1, chips):
                forward(side, j, d).wait_send()
        sib_copy(j).wait_send()
        for d in range(1, chips):
            cross_copy(j, d).wait_send()
        for kind in range(4):
            out_copy(kind, j).wait()
        return carry

    lax.fori_loop(0, KVH, drain, 0)
    for step in range(1, members):
        stat_copy(step).wait_send()
    for step in range(1, groups):
        tok_copy(step).wait_send()
    for copy in ends:
        copy.wait()


def place_kernel(*refs):
    count = (len(refs) - 1) // 2
    copies = [pltpu.make_async_copy(refs[i], refs[count + i], refs[-1].at[i]) for i in range(count)]
    for copy in copies:
        copy.start()
    for copy in copies:
        copy.wait()


def body(prompt_k, prompt_v, resp_q, resp_k, resp_v, out_grad, lengths, rewards):
    members = lax.axis_size("member")
    groups = lax.axis_size("group")
    chips = members // 2
    rows = prompt_k.shape[1]
    slots = resp_q.shape[2]
    per_head = resp_q.shape[3] // (KVH * HD)
    keys = members * rows + slots
    width = KVH * HD
    bf, f32 = jnp.bfloat16, jnp.float32
    dma = pltpu.SemaphoreType.DMA
    crossing = max(chips - 1, 1)
    scratch = [
        pltpu.VMEM((keys, width), bf),
        pltpu.VMEM((keys, width), bf),
        pltpu.VMEM((slots, width * per_head), bf),
        pltpu.VMEM((slots, width * per_head), bf),
        pltpu.VMEM((slots, width * per_head), bf),
        pltpu.VMEM((slots, width * per_head), bf),
        pltpu.VMEM((slots, width), f32),
        pltpu.VMEM((slots, width), f32),
        pltpu.VMEM((slots, width), bf),
        pltpu.VMEM((slots, width), bf),
        pltpu.VMEM((rows, width), bf),
        pltpu.VMEM((rows, width), bf),
        pltpu.VMEM((keys, slots * per_head), bf),
        pltpu.VMEM((keys, slots * per_head), bf),
        pltpu.VMEM((keys, slots * per_head), bf),
        pltpu.VMEM((keys, slots * per_head), bf),
        pltpu.VMEM((KVH, members, rows, 2 * HD), f32),
        pltpu.VMEM((KVH, chips, rows, 2 * HD), bf),
        pltpu.VMEM((KVH, chips, rows, 2 * HD), bf),
        pltpu.VMEM((KVH, crossing, rows, 2 * HD), bf),
        pltpu.VMEM((KVH, crossing, rows, 2 * HD), bf),
        pltpu.VMEM((2, 8, HD), f32),
        pltpu.VMEM((members, 2, 8, HD), f32),
        pltpu.VMEM((8, HD), f32),
        pltpu.VMEM((groups, 8, HD), f32),
        dma((6,)),
        dma((2, KVH, chips)),
        dma((2, KVH, crossing)),
        dma((2, KVH, members)),
        dma((members,)),
        dma((members,)),
        dma((groups,)),
        dma((groups,)),
        dma((KVH,)),
        dma((KVH,)),
        dma((KVH, crossing)),
        dma((KVH, crossing)),
        dma((4, KVH)),
        dma((2,)),
    ]
    held = pl.BlockSpec(memory_space=pl.ANY)
    scalar = pl.BlockSpec(memory_space=pltpu.SMEM)
    stored = pl.BlockSpec(memory_space=pltpu.HBM)
    flops = 10 * slots * width * per_head * keys
    moved = sum(2 * a.size * a.dtype.itemsize for a in (resp_q, out_grad, resp_k, resp_v, prompt_k, prompt_v))
    results = pl.pallas_call(
        functools.partial(kernel, groups, members, rows, slots, per_head),
        out_shape=[
            jax.ShapeDtypeStruct(a.shape, bf) for a in (resp_q, resp_q, resp_k, resp_v, prompt_k, prompt_v)
        ],
        in_specs=[scalar, scalar] + [stored] * 6,
        out_specs=[held] * 6,
        scratch_shapes=scratch,
        compiler_params=pltpu.CompilerParams(
            collective_id=0, has_side_effects=True, vmem_limit_bytes=60 * 1024 * 1024),
        cost_estimate=pl.CostEstimate(
            flops=flops, bytes_accessed=moved, transcendentals=slots * KVH * per_head * keys),
        name="shared_prompt_attention",
    )(lengths, rewards, prompt_k, prompt_v, resp_q, resp_k, resp_v, out_grad)
    return pl.pallas_call(
        place_kernel,
        out_shape=[jax.ShapeDtypeStruct(a.shape, bf) for a in results],
        in_specs=[held] * 6,
        out_specs=[stored] * 6,
        scratch_shapes=[dma((6,))],
        compiler_params=pltpu.CompilerParams(vmem_limit_bytes=60 * 1024 * 1024),
        cost_estimate=pl.CostEstimate(flops=0, bytes_accessed=moved, transcendentals=0),
        name="place_results",
    )(*results)


def solution(mesh):
    rows = P("group", "member", None)
    wide = P("group", "member", None, None)
    return jax.shard_map(
        body,
        mesh=mesh,
        in_specs=(rows, rows, wide, wide, wide, wide, P("group", "member"), P("group", "member")),
        out_specs=(wide, wide, wide, wide, rows, rows),
        check_vma=False,
    )
```

```python
import functools

import jax
import jax.numpy as jnp
from jax import lax
from jax.experimental import pallas as pl
from jax.experimental.pallas import tpu as pltpu
from jax.sharding import PartitionSpec as P

KVH = 8
HD = 128
LOG2E = 1.4426950408889634
MESH = pl.DeviceIdType.MESH
NT = (((1,), (1,)), ((), ()))
NN = (((1,), (0,)), ((), ()))
TN = (((0,), (0,)), ((), ()))


def dot(a, b, dims):
    return lax.dot_general(a, b, dims, preferred_element_type=jnp.float32)


def kernel(
    groups, members, rows, slots, per_head,
    length_ref, reward_ref, pk_ref, pv_ref, q_ref, rk_ref, rv_ref, og_ref,
    att_out, gq_out, grk_out, grv_out, gpk_out, gpv_out,
    kall, vall, qbuf, obuf, att, gq, grk, grv, grk_low, grv_low, gpk, gpv,
    probs0, probs1, dsc0, dsc1,
    part, sib_send, sib_recv, x_send, x_recv, stat_send, stat, tok_send, tok,
    in_sem, g_send, f_send, g_recv, s_send, s_recv, t_send, t_recv,
    r_send, r_recv, c_send, c_recv, out_sem, end_sem,
):
    chips = members // 2
    prompt = members * rows
    wide = per_head * slots
    score_scale = float(HD) ** (-0.5)
    group = lax.axis_index("group")
    me = lax.axis_index("member")
    chip = lax.div(me, 2)
    core = lax.rem(me, 2)
    sib = chip * 2 + (1 - core)

    def chip_at(d):
        return lax.rem(chip + d, chips)

    def cols(j, width=HD):
        return pl.ds(pl.multiple_of(j * width, width), width)

    def block_rows(owner):
        return pl.ds(pl.multiple_of(owner * rows, rows), rows)

    def local(src, dst, sem):
        return pltpu.make_async_copy(src, dst, sem)

    def remote(src, dst, send, recv, to_group, to_member):
        return pltpu.make_async_remote_copy(
            src_ref=src, dst_ref=dst, send_sem=send, recv_sem=recv,
            device_id=(to_group, to_member), device_id_type=MESH)

    loads = [
        local(pk_ref.at[0], kall.at[block_rows(me)], in_sem.at[0]),
        local(pv_ref.at[0], vall.at[block_rows(me)], in_sem.at[1]),
        local(rk_ref.at[0, 0], kall.at[pl.ds(prompt, slots)], in_sem.at[2]),
        local(rv_ref.at[0, 0], vall.at[pl.ds(prompt, slots)], in_sem.at[3]),
        local(q_ref.at[0, 0], qbuf, in_sem.at[4]),
        local(og_ref.at[0, 0], obuf, in_sem.at[5]),
    ]
    for load in loads:
        load.start()

    barrier = pltpu.get_barrier_semaphore()
    for step in range(1, members):
        pl.semaphore_signal(barrier, inc=1, device_id=(group, lax.rem(me + step, members)), device_id_type=MESH)
    nodes = groups // 2
    node = lax.div(group, 2)
    twin = node * 2 + (1 - lax.rem(group, 2))
    pl.semaphore_signal(barrier, inc=1, device_id=(twin, me), device_id_type=MESH)

    @pl.when(node > 0)
    def _():
        pl.semaphore_signal(barrier, inc=1, device_id=(group - 2, me), device_id_type=MESH)

    @pl.when(node < nodes - 1)
    def _():
        pl.semaphore_signal(barrier, inc=1, device_id=(group + 2, me), device_id_type=MESH)


    length = length_ref[0, 0]
    stat_send[0] = jnp.full((8, HD), length.astype(jnp.float32))
    stat_send[1] = jnp.full((8, HD), reward_ref[0, 0])
    stat[me] = stat_send[...]
    ends = (node == 0).astype(jnp.int32) + (node == nodes - 1).astype(jnp.int32)
    pl.semaphore_wait(barrier, members + 2 - ends)

    sides = ((pk_ref, kall), (pv_ref, vall))

    def direct(side, j, slot):
        to = sib if slot == 0 else chip_at(slot) * 2 + core
        source, whole = sides[side]
        return remote(source.at[0, :, cols(j)], whole.at[block_rows(me), cols(j)],
                      g_send.at[side, j, slot], g_recv.at[side, j, me], group, to)

    def arrival(side, j, owner):
        place = sides[side][1].at[block_rows(owner), cols(j)]
        return remote(place, place, g_send.at[side, j, 0], g_recv.at[side, j, owner], group, sib)

    def forward(side, j, d):
        owner = chip_at(d) * 2 + core
        place = sides[side][1].at[block_rows(owner), cols(j)]
        return remote(place, place, f_send.at[side, j, d - 1], g_recv.at[side, j, owner], group, sib)

    def stat_copy(step):
        return remote(stat_send, stat.at[me], s_send.at[step - 1], s_recv.at[me], group, lax.rem(me + step, members))

    def tok_copy(kind):
        to = (twin, group + 2, group - 2)[kind]
        return remote(tok_send.at[kind], tok.at[kind], t_send.at[kind], t_recv.at[kind], to, me)

    def relay(slot):
        @pl.when(node == slot)
        def _():
            @pl.when(node > 0)
            def _():
                tok_copy(1).wait_recv()
                tok_send[1] = tok[1] + tok[3]

            @pl.when(node == 0)
            def _():
                tok_send[1] = tok[3]

            @pl.when(node < nodes - 1)
            def _():
                tok_copy(1).start()

        @pl.when(node == nodes - 1 - slot)
        def _():
            @pl.when(node < nodes - 1)
            def _():
                tok_copy(2).wait_recv()
                tok_send[2] = tok[2] + tok[3]

            @pl.when(node == nodes - 1)
            def _():
                tok_send[2] = tok[3]

            @pl.when(node > 0)
            def _():
                tok_copy(2).start()

    def far(side, d):
        source, whole = sides[side]
        return remote(source.at[0, :, cols(0)], whole.at[block_rows(me), cols(0)],
                      f_send.at[side, 0, d - 1], g_recv.at[side, 0, me], group, chip_at(d) * 2 + (1 - core))

    def send_head(j, carry):
        for slot in list(range(1, chips)) + [0]:
            for side in range(2):
                direct(side, j, slot).start()
        return carry

    send_head(0, 0)
    for d in range(1, chips):
        for side in range(2):
            far(side, d).start()
    for step in range(1, members):
        stat_copy(step).start()
    lax.fori_loop(1, KVH, send_head, 0)

    def forward_head(j):
        for d in range(1, chips):
            owner = chip_at(d) * 2 + core
            for side in range(2):
                arrival(side, j, owner).wait_recv()
                forward(side, j, d).start()

    def wait_head(j):
        for side in range(2):
            arrival(side, j, sib).wait_recv()
            for d in range(1, chips):
                arrival(side, j, chip_at(d) * 2 + (1 - core)).wait_recv()

    u_pos = lax.broadcasted_iota(jnp.int32, (slots, wide), 0)
    t_pos = lax.rem(lax.broadcasted_iota(jnp.int32, (slots, wide), 1), slots)
    causal = u_pos <= t_pos
    live_lane = lax.rem(lax.broadcasted_iota(jnp.int32, (HD, wide), 1), slots) < length
    live_row = lax.broadcasted_iota(jnp.int32, (slots, per_head * HD), 0) < length

    for load in loads:
        load.wait()

    def mask_head(j, carry):
        g = obuf[:, cols(j, per_head * HD)]
        obuf[:, cols(j, per_head * HD)] = jnp.where(live_row, g, jnp.zeros_like(g))
        return carry

    lax.fori_loop(0, KVH, mask_head, 0)

    def sib_copy(j):
        return remote(sib_send.at[j], sib_recv.at[j], r_send.at[j], r_recv.at[j], group, sib)

    def cross_copy(j, d):
        return remote(x_send.at[j, d - 1], x_recv.at[j, d - 1], c_send.at[j, d - 1], c_recv.at[j, d - 1],
                      group, chip_at(d) * 2 + core)

    def cross_head(j):
        sib_copy(j).wait_recv()
        for d in range(1, chips):
            own = part[j, chip_at(d) * 2 + core]
            x_send[j, d - 1] = (own + sib_recv[j, d].astype(jnp.float32)).astype(jnp.bfloat16)
            cross_copy(j, d).start()

    def out_copy(kind, j):
        held, out, width = ((att, att_out, per_head * HD), (gq, gq_out, per_head * HD),
                            (grk_low, grk_out, HD), (grv_low, grv_out, HD))[kind]
        return local(held.at[:, cols(j, width)], out.at[0, 0, :, cols(j, width)], out_sem.at[kind, j])

    def stacked(buf, j):
        return jnp.concatenate([buf[:, cols(j * per_head + h)] for h in range(per_head)], axis=0)

    def heads(back, fore, back_bufs, fore_bufs):
        if fore is not None:
            s = dot(kall[:, cols(fore)], stacked(qbuf, fore), NT)
        if back is not None:
            p_back = back_bufs[0][...]
            dv = dot(p_back, stacked(obuf, back), NN) * adv_row
            o_t = dot(vall[:, cols(back)], p_back, TN)
        if fore is not None:
            s = jnp.concatenate([s[:prompt], jnp.where(causal, s[prompt:], -1e30)], axis=0)
            top = jnp.max(s, axis=0, keepdims=True)
            e = jnp.exp2((s - top) * (score_scale * LOG2E))
            p = e * (1.0 / jnp.sum(e, axis=0, keepdims=True))
            fore_bufs[0][...] = p.astype(jnp.bfloat16)
            dp = dot(vall[:, cols(fore)], stacked(obuf, fore), NT)
        if back is not None:
            ds_back = back_bufs[1][...]
            dk = dot(ds_back, stacked(qbuf, back), NN) * (adv_row * score_scale)
            dq_t = dot(kall[:, cols(back)], ds_back, TN) * (adv_one * score_scale)
        if fore is not None:
            delta = jnp.sum(p * dp, axis=0, keepdims=True)
            fore_bufs[1][...] = (p * (dp - delta)).astype(jnp.bfloat16)
        if back is not None:
            part[back, :, :, :HD] = dk[:prompt].reshape(members, rows, HD)
            part[back, :, :, HD:] = dv[:prompt].reshape(members, rows, HD)
            for d in range(chips):
                sib_send[back, d] = part[back, chip_at(d) * 2 + (1 - core)].astype(jnp.bfloat16)
            sib_copy(back).start()
            grk[:, cols(back)] = dk[prompt:]
            grv[:, cols(back)] = dv[prompt:]
            o_t = jnp.where(live_lane, o_t, 0.0).astype(jnp.bfloat16)
            dq_t = dq_t.astype(jnp.bfloat16)
            for h in range(per_head):
                att[:, cols(back * per_head + h)] = o_t[:, h * slots:(h + 1) * slots].T
                gq[:, cols(back * per_head + h)] = dq_t[:, h * slots:(h + 1) * slots].T
            out_copy(0, back).start()

    bufs = ((probs0, dsc0), (probs1, dsc1))
    wait_head(0)
    for side in range(2):
        for d in range(1, chips):
            arrival(side, 0, chip_at(d) * 2 + core).wait_recv()
    forward_head(1)
    heads(None, 0, None, bufs[0])
    for step in range(1, members):
        owner = lax.rem(me + step, members)
        remote(stat_send, stat.at[owner], s_send.at[0], s_recv.at[owner], group, owner).wait_recv()
    tok_send[0] = functools.reduce(jnp.add, [stat[i, 0] for i in range(members)])
    tok_copy(0).start()
    reward_total = functools.reduce(jnp.add, [stat[i, 1] for i in range(members)])
    advantage = stat_send[1] - reward_total / members
    adv_row = advantage[0:1]
    adv_one = adv_row[:, 0:1]

    def pair(i, carry):
        j = 2 * i
        forward_head(j + 2)
        wait_head(j + 1)
        heads(j, j + 1, bufs[0], bufs[1])

        @pl.when(i > 0)
        def _():
            cross_head(j - 1)

        @pl.when(i == 0)
        def _():
            tok_copy(0).wait_recv()
            tok[3] = tok_send[0] + tok[0]

        relay(j)
        forward_head(j + 3)
        wait_head(j + 2)
        heads(j + 1, j + 2, bufs[1], bufs[0])
        cross_head(j)
        relay(j + 1)
        return carry

    lax.fori_loop(0, KVH // 2 - 1, pair, 0)
    wait_head(KVH - 1)
    heads(KVH - 2, KVH - 1, bufs[0], bufs[1])
    cross_head(KVH - 3)
    heads(KVH - 1, None, bufs[1], None)
    cross_head(KVH - 2)
    for slot in range(KVH - 2, nodes):
        relay(slot)
    tokens = tok[3]
    before = jnp.where(node > 0, tok_send[1] - tok[3], jnp.zeros_like(tokens))
    after = jnp.where(node < nodes - 1, tok_send[2] - tok[3], jnp.zeros_like(tokens))
    tokens = tokens + before + after
    factor = (float(slots * groups * members) / tokens)[0:1]
    factor_one = factor[:, 0:1]

    def scale_head(j, carry):
        span = cols(j, per_head * HD)
        gq[:, span] = (gq[:, span].astype(jnp.float32) * factor_one).astype(jnp.bfloat16)
        grk_low[:, cols(j)] = (grk[:, cols(j)] * factor).astype(jnp.bfloat16)
        grv_low[:, cols(j)] = (grv[:, cols(j)] * factor).astype(jnp.bfloat16)
        for kind in range(1, 4):
            out_copy(kind, j).start()
        return carry

    lax.fori_loop(0, KVH // 2, scale_head, 0)
    cross_head(KVH - 1)
    lax.fori_loop(KVH // 2, KVH, scale_head, 0)

    def finish(j, carry):
        total = part[j, me] + sib_recv[j, 0].astype(jnp.float32)
        for d in range(1, chips):
            cross_copy(j, d).wait_recv()
            total = total + x_recv[j, d - 1].astype(jnp.float32)
        gpk[:, cols(j)] = (total[:, :HD] * factor).astype(jnp.bfloat16)
        gpv[:, cols(j)] = (total[:, HD:] * factor).astype(jnp.bfloat16)
        return carry

    lax.fori_loop(0, KVH, finish, 0)
    ends = [local(gpk, gpk_out.at[0], end_sem.at[0]), local(gpv, gpv_out.at[0], end_sem.at[1])]
    for copy in ends:
        copy.start()

    def drain(j, carry):
        for side in range(2):
            for slot in range(chips):
                direct(side, j, slot).wait_send()
            for d in range(1, chips):
                forward(side, j, d).wait_send()
        sib_copy(j).wait_send()
        for d in range(1, chips):
            cross_copy(j, d).wait_send()
        for kind in range(4):
            out_copy(kind, j).wait()
        return carry

    lax.fori_loop(0, KVH, drain, 0)
    for step in range(1, members):
        stat_copy(step).wait_send()
    tok_copy(0).wait_send()

    @pl.when(node < nodes - 1)
    def _():
        tok_copy(1).wait_send()

    @pl.when(node > 0)
    def _():
        tok_copy(2).wait_send()

    for copy in ends:
        copy.wait()


def place_kernel(*refs):
    count = len(refs) // 3
    sem = refs[-1]
    ins, outs = [], []
    for i in range(count):
        source, out, held = refs[i], refs[count + i], refs[2 * count + i]
        tall = source.shape[-2]
        pieces = 2 if source.shape[-1] > KVH * HD else 1
        for piece in range(pieces):
            span = pl.ds(piece * (tall // pieces), tall // pieces)
            index = (0,) * (len(source.shape) - 2) + (span,)
            spot = len(ins)
            ins.append(pltpu.make_async_copy(source.at[index], held.at[span], sem.at[0, spot]))
            outs.append(pltpu.make_async_copy(held.at[span], out.at[index], sem.at[1, spot]))
    for copy in ins:
        copy.start()
    for copy_in, copy_out in zip(ins, outs):
        copy_in.wait()
        copy_out.start()
    for copy in outs:
        copy.wait()


def body(prompt_k, prompt_v, resp_q, resp_k, resp_v, out_grad, lengths, rewards):
    members = lax.axis_size("member")
    groups = lax.axis_size("group")
    chips = members // 2
    rows = prompt_k.shape[1]
    slots = resp_q.shape[2]
    per_head = resp_q.shape[3] // (KVH * HD)
    keys = members * rows + slots
    width = KVH * HD
    bf, f32 = jnp.bfloat16, jnp.float32
    dma = pltpu.SemaphoreType.DMA
    crossing = max(chips - 1, 1)
    scratch = [
        pltpu.VMEM((keys, width), bf),
        pltpu.VMEM((keys, width), bf),
        pltpu.VMEM((slots, width * per_head), bf),
        pltpu.VMEM((slots, width * per_head), bf),
        pltpu.VMEM((slots, width * per_head), bf),
        pltpu.VMEM((slots, width * per_head), bf),
        pltpu.VMEM((slots, width), f32),
        pltpu.VMEM((slots, width), f32),
        pltpu.VMEM((slots, width), bf),
        pltpu.VMEM((slots, width), bf),
        pltpu.VMEM((rows, width), bf),
        pltpu.VMEM((rows, width), bf),
        pltpu.VMEM((keys, slots * per_head), bf),
        pltpu.VMEM((keys, slots * per_head), bf),
        pltpu.VMEM((keys, slots * per_head), bf),
        pltpu.VMEM((keys, slots * per_head), bf),
        pltpu.VMEM((KVH, members, rows, 2 * HD), f32),
        pltpu.VMEM((KVH, chips, rows, 2 * HD), bf),
        pltpu.VMEM((KVH, chips, rows, 2 * HD), bf),
        pltpu.VMEM((KVH, crossing, rows, 2 * HD), bf),
        pltpu.VMEM((KVH, crossing, rows, 2 * HD), bf),
        pltpu.VMEM((2, 8, HD), f32),
        pltpu.VMEM((members, 2, 8, HD), f32),
        pltpu.VMEM((3, 8, HD), f32),
        pltpu.VMEM((4, 8, HD), f32),
        dma((6,)),
        dma((2, KVH, chips)),
        dma((2, KVH, crossing)),
        dma((2, KVH, members)),
        dma((members,)),
        dma((members,)),
        dma((3,)),
        dma((3,)),
        dma((KVH,)),
        dma((KVH,)),
        dma((KVH, crossing)),
        dma((KVH, crossing)),
        dma((4, KVH)),
        dma((2,)),
    ]
    held = pl.BlockSpec(memory_space=pl.ANY)
    scalar = pl.BlockSpec(memory_space=pltpu.SMEM)
    stored = pl.BlockSpec(memory_space=pltpu.HBM)
    flops = 10 * slots * width * per_head * keys
    moved = sum(2 * a.size * a.dtype.itemsize for a in (resp_q, out_grad, resp_k, resp_v, prompt_k, prompt_v))
    results = pl.pallas_call(
        functools.partial(kernel, groups, members, rows, slots, per_head),
        out_shape=[
            jax.ShapeDtypeStruct(a.shape, bf) for a in (resp_q, resp_q, resp_k, resp_v, prompt_k, prompt_v)
        ],
        in_specs=[scalar, scalar] + [stored] * 6,
        out_specs=[held] * 6,
        scratch_shapes=scratch,
        compiler_params=pltpu.CompilerParams(
            collective_id=0, has_side_effects=True, vmem_limit_bytes=60 * 1024 * 1024),
        cost_estimate=pl.CostEstimate(
            flops=flops, bytes_accessed=moved, transcendentals=slots * KVH * per_head * keys),
        name="shared_prompt_attention",
    )(lengths, rewards, prompt_k, prompt_v, resp_q, resp_k, resp_v, out_grad)
    return pl.pallas_call(
        place_kernel,
        out_shape=[jax.ShapeDtypeStruct(a.shape, bf) for a in results],
        in_specs=[stored] * 6,
        out_specs=[stored] * 6,
        scratch_shapes=[pltpu.VMEM(a.shape[-2:], bf) for a in results] + [dma((2, 8))],
        compiler_params=pltpu.CompilerParams(vmem_limit_bytes=60 * 1024 * 1024),
        cost_estimate=pl.CostEstimate(flops=0, bytes_accessed=moved, transcendentals=0),
        name="place_results",
    )(*results)


def solution(mesh):
    rows = P("group", "member", None)
    wide = P("group", "member", None, None)
    return jax.shard_map(
        body,
        mesh=mesh,
        in_specs=(rows, rows, wide, wide, wide, wide, P("group", "member"), P("group", "member")),
        out_specs=(wide, wide, wide, wide, rows, rows),
        check_vma=False,
    )
```

```python
import functools

import jax
import jax.numpy as jnp
from jax import lax
from jax.experimental import pallas as pl
from jax.experimental.pallas import tpu as pltpu
from jax.sharding import PartitionSpec as P

KVH = 8
HD = 128
LOG2E = 1.4426950408889634
MESH = pl.DeviceIdType.MESH
NT = (((1,), (1,)), ((), ()))
NN = (((1,), (0,)), ((), ()))
TN = (((0,), (0,)), ((), ()))


def dot(a, b, dims):
    return lax.dot_general(a, b, dims, preferred_element_type=jnp.float32)


def kernel(
    groups, members, rows, slots, per_head,
    length_ref, reward_ref, pk_ref, pv_ref, q_ref, rk_ref, rv_ref, og_ref,
    att_out, gq_out, grk_out, grv_out, gpk_out, gpv_out,
    kall, vall, qbuf, obuf, att, gq, grk, grv, grk_low, grv_low, gpk, gpv,
    probs0, probs1, dsc0, dsc1,
    part, sib_send, sib_recv, x_send, x_recv, stat_send, stat, tok_send, tok,
    in_sem, g_send, f_send, g_recv, s_send, s_recv, t_send, t_recv,
    r_send, r_recv, c_send, c_recv, out_sem, end_sem,
):
    chips = members // 2
    prompt = members * rows
    wide = per_head * slots
    score_scale = float(HD) ** (-0.5)
    group = lax.axis_index("group")
    me = lax.axis_index("member")
    chip = lax.div(me, 2)
    core = lax.rem(me, 2)
    sib = chip * 2 + (1 - core)

    def chip_at(d):
        return lax.rem(chip + d, chips)

    def cols(j, width=HD):
        return pl.ds(pl.multiple_of(j * width, width), width)

    def block_rows(owner):
        return pl.ds(pl.multiple_of(owner * rows, rows), rows)

    def local(src, dst, sem):
        return pltpu.make_async_copy(src, dst, sem)

    def remote(src, dst, send, recv, to_group, to_member):
        return pltpu.make_async_remote_copy(
            src_ref=src, dst_ref=dst, send_sem=send, recv_sem=recv,
            device_id=(to_group, to_member), device_id_type=MESH)

    loads = [
        local(pk_ref.at[0], kall.at[block_rows(me)], in_sem.at[0]),
        local(pv_ref.at[0], vall.at[block_rows(me)], in_sem.at[1]),
        local(rk_ref.at[0, 0], kall.at[pl.ds(prompt, slots)], in_sem.at[2]),
        local(rv_ref.at[0, 0], vall.at[pl.ds(prompt, slots)], in_sem.at[3]),
        local(q_ref.at[0, 0], qbuf, in_sem.at[4]),
        local(og_ref.at[0, 0], obuf, in_sem.at[5]),
    ]
    for load in loads:
        load.start()

    barrier = pltpu.get_barrier_semaphore()
    for step in range(1, members):
        pl.semaphore_signal(barrier, inc=1, device_id=(group, lax.rem(me + step, members)), device_id_type=MESH)
    nodes = groups // 2
    node = lax.div(group, 2)
    twin = node * 2 + (1 - lax.rem(group, 2))
    pl.semaphore_signal(barrier, inc=1, device_id=(twin, me), device_id_type=MESH)

    @pl.when(node > 0)
    def _():
        pl.semaphore_signal(barrier, inc=1, device_id=(group - 2, me), device_id_type=MESH)

    @pl.when(node < nodes - 1)
    def _():
        pl.semaphore_signal(barrier, inc=1, device_id=(group + 2, me), device_id_type=MESH)


    length = length_ref[0, 0]
    stat_send[0] = jnp.full((8, HD), length.astype(jnp.float32))
    stat_send[1] = jnp.full((8, HD), reward_ref[0, 0])
    stat[me] = stat_send[...]
    ends = (node == 0).astype(jnp.int32) + (node == nodes - 1).astype(jnp.int32)
    pl.semaphore_wait(barrier, members + 2 - ends)

    sides = ((pk_ref, kall), (pv_ref, vall))

    def direct(side, j, slot):
        to = sib if slot == 0 else chip_at(slot) * 2 + core
        source, whole = sides[side]
        return remote(source.at[0, :, cols(j)], whole.at[block_rows(me), cols(j)],
                      g_send.at[side, j, slot], g_recv.at[side, j, me], group, to)

    def arrival(side, j, owner):
        place = sides[side][1].at[block_rows(owner), cols(j)]
        return remote(place, place, g_send.at[side, j, 0], g_recv.at[side, j, owner], group, sib)

    def forward(side, j, d):
        owner = chip_at(d) * 2 + core
        place = sides[side][1].at[block_rows(owner), cols(j)]
        return remote(place, place, f_send.at[side, j, d - 1], g_recv.at[side, j, owner], group, sib)

    def stat_copy(step):
        return remote(stat_send, stat.at[me], s_send.at[step - 1], s_recv.at[me], group, lax.rem(me + step, members))

    def tok_copy(kind):
        to = (twin, group + 2, group - 2)[kind]
        return remote(tok_send.at[kind], tok.at[kind], t_send.at[kind], t_recv.at[kind], to, me)

    def relay(slot):
        @pl.when(2 * node == slot)
        def _():
            @pl.when(node > 0)
            def _():
                tok_copy(1).wait_recv()
                tok_send[1] = tok[1] + tok[3]

            @pl.when(node == 0)
            def _():
                tok_send[1] = tok[3]

            @pl.when(node < nodes - 1)
            def _():
                tok_copy(1).start()

        @pl.when(2 * (nodes - 1 - node) == slot)
        def _():
            @pl.when(node < nodes - 1)
            def _():
                tok_copy(2).wait_recv()
                tok_send[2] = tok[2] + tok[3]

            @pl.when(node == nodes - 1)
            def _():
                tok_send[2] = tok[3]

            @pl.when(node > 0)
            def _():
                tok_copy(2).start()

    def far(side, d):
        source, whole = sides[side]
        return remote(source.at[0, :, cols(0)], whole.at[block_rows(me), cols(0)],
                      f_send.at[side, 0, d - 1], g_recv.at[side, 0, me], group, chip_at(d) * 2 + (1 - core))

    def send_head(j, carry):
        for slot in list(range(1, chips)) + [0]:
            for side in range(2):
                direct(side, j, slot).start()
        return carry

    send_head(0, 0)
    for d in range(1, chips):
        for side in range(2):
            far(side, d).start()
    for step in range(1, members):
        stat_copy(step).start()
    lax.fori_loop(1, KVH, send_head, 0)

    def forward_head(j):
        for d in range(1, chips):
            owner = chip_at(d) * 2 + core
            for side in range(2):
                arrival(side, j, owner).wait_recv()
                forward(side, j, d).start()

    def wait_head(j):
        for side in range(2):
            arrival(side, j, sib).wait_recv()
            for d in range(1, chips):
                arrival(side, j, chip_at(d) * 2 + (1 - core)).wait_recv()

    u_pos = lax.broadcasted_iota(jnp.int32, (slots, wide), 0)
    t_pos = lax.rem(lax.broadcasted_iota(jnp.int32, (slots, wide), 1), slots)
    causal = u_pos <= t_pos
    live_lane = lax.rem(lax.broadcasted_iota(jnp.int32, (HD, wide), 1), slots) < length
    live_row = lax.broadcasted_iota(jnp.int32, (slots, per_head * HD), 0) < length

    for load in loads:
        load.wait()

    def mask_head(j, carry):
        g = obuf[:, cols(j, per_head * HD)]
        obuf[:, cols(j, per_head * HD)] = jnp.where(live_row, g, jnp.zeros_like(g))
        return carry

    lax.fori_loop(0, KVH, mask_head, 0)

    def sib_copy(j):
        return remote(sib_send.at[j], sib_recv.at[j], r_send.at[j], r_recv.at[j], group, sib)

    def cross_copy(j, d):
        return remote(x_send.at[j, d - 1], x_recv.at[j, d - 1], c_send.at[j, d - 1], c_recv.at[j, d - 1],
                      group, chip_at(d) * 2 + core)

    def send_part(j):
        for d in range(chips):
            sib_send[j, d] = part[j, chip_at(d) * 2 + (1 - core)].astype(jnp.bfloat16)
        sib_copy(j).start()

    def cross_head(j):
        sib_copy(j).wait_recv()
        for d in range(1, chips):
            own = part[j, chip_at(d) * 2 + core]
            x_send[j, d - 1] = (own + sib_recv[j, d].astype(jnp.float32)).astype(jnp.bfloat16)
            cross_copy(j, d).start()

    def out_copy(kind, j):
        held, out, width = ((att, att_out, per_head * HD), (gq, gq_out, per_head * HD),
                            (grk_low, grk_out, HD), (grv_low, grv_out, HD))[kind]
        return local(held.at[:, cols(j, width)], out.at[0, 0, :, cols(j, width)], out_sem.at[kind, j])

    def stacked(buf, j):
        return jnp.concatenate([buf[:, cols(j * per_head + h)] for h in range(per_head)], axis=0)

    def heads(back, fore, back_bufs, fore_bufs):
        if fore is not None:
            s = dot(kall[:, cols(fore)], stacked(qbuf, fore), NT)
        if back is not None:
            p_back = back_bufs[0][...]
            dv = dot(p_back, stacked(obuf, back), NN) * adv_row
            o_t = dot(vall[:, cols(back)], p_back, TN)
        if fore is not None:
            s = jnp.concatenate([s[:prompt], jnp.where(causal, s[prompt:], -1e30)], axis=0)
            top = jnp.max(s, axis=0, keepdims=True)
            e = jnp.exp2((s - top) * (score_scale * LOG2E))
            p = e * (1.0 / jnp.sum(e, axis=0, keepdims=True))
            fore_bufs[0][...] = p.astype(jnp.bfloat16)
            dp = dot(vall[:, cols(fore)], stacked(obuf, fore), NT)
        if back is not None:
            ds_back = back_bufs[1][...]
            dk = dot(ds_back, stacked(qbuf, back), NN) * (adv_row * score_scale)
            dq_t = dot(kall[:, cols(back)], ds_back, TN) * (adv_one * score_scale)
        if fore is not None:
            delta = jnp.sum(p * dp, axis=0, keepdims=True)
            fore_bufs[1][...] = (p * (dp - delta)).astype(jnp.bfloat16)
        if back is not None:
            part[back, :, :, :HD] = dk[:prompt].reshape(members, rows, HD)
            part[back, :, :, HD:] = dv[:prompt].reshape(members, rows, HD)
            if fore is None:
                send_part(back)
            grk[:, cols(back)] = dk[prompt:]
            grv[:, cols(back)] = dv[prompt:]
            o_t = jnp.where(live_lane, o_t, 0.0).astype(jnp.bfloat16)
            dq_t = dq_t.astype(jnp.bfloat16)
            for h in range(per_head):
                att[:, cols(back * per_head + h)] = o_t[:, h * slots:(h + 1) * slots].T
                gq[:, cols(back * per_head + h)] = dq_t[:, h * slots:(h + 1) * slots].T
            if fore is not None:
                send_part(back)
            out_copy(0, back).start()

    bufs = ((probs0, dsc0), (probs1, dsc1))
    wait_head(0)
    for side in range(2):
        for d in range(1, chips):
            arrival(side, 0, chip_at(d) * 2 + core).wait_recv()
    forward_head(1)
    heads(None, 0, None, bufs[0])
    for step in range(1, members):
        owner = lax.rem(me + step, members)
        remote(stat_send, stat.at[owner], s_send.at[0], s_recv.at[owner], group, owner).wait_recv()
    tok_send[0] = functools.reduce(jnp.add, [stat[i, 0] for i in range(members)])
    tok_copy(0).start()
    reward_total = functools.reduce(jnp.add, [stat[i, 1] for i in range(members)])
    advantage = stat_send[1] - reward_total / members
    adv_row = advantage[0:1]
    adv_one = adv_row[:, 0:1]

    def pair(i, carry):
        j = 2 * i
        forward_head(j + 2)
        wait_head(j + 1)
        heads(j, j + 1, bufs[0], bufs[1])

        @pl.when(i > 0)
        def _():
            cross_head(j - 1)

        @pl.when(i == 0)
        def _():
            tok_copy(0).wait_recv()
            tok[3] = tok_send[0] + tok[0]

        relay(j)
        forward_head(j + 3)
        wait_head(j + 2)
        heads(j + 1, j + 2, bufs[1], bufs[0])
        cross_head(j)
        relay(j + 1)
        return carry

    lax.fori_loop(0, KVH // 2 - 1, pair, 0)
    wait_head(KVH - 1)
    heads(KVH - 2, KVH - 1, bufs[0], bufs[1])
    cross_head(KVH - 3)
    heads(KVH - 1, None, bufs[1], None)
    cross_head(KVH - 2)
    for slot in range(KVH - 2, 2 * nodes - 1):
        relay(slot)
    tokens = tok[3]
    before = jnp.where(node > 0, tok_send[1] - tok[3], jnp.zeros_like(tokens))
    after = jnp.where(node < nodes - 1, tok_send[2] - tok[3], jnp.zeros_like(tokens))
    tokens = tokens + before + after
    factor = (float(slots * groups * members) / tokens)[0:1]
    factor_one = factor[:, 0:1]

    def scale_head(j, carry):
        span = cols(j, per_head * HD)
        gq[:, span] = (gq[:, span].astype(jnp.float32) * factor_one).astype(jnp.bfloat16)
        grk_low[:, cols(j)] = (grk[:, cols(j)] * factor).astype(jnp.bfloat16)
        grv_low[:, cols(j)] = (grv[:, cols(j)] * factor).astype(jnp.bfloat16)
        for kind in range(1, 4):
            out_copy(kind, j).start()
        return carry

    lax.fori_loop(0, KVH // 2, scale_head, 0)
    cross_head(KVH - 1)
    lax.fori_loop(KVH // 2, KVH, scale_head, 0)

    def finish(j, carry):
        total = part[j, me] + sib_recv[j, 0].astype(jnp.float32)
        for d in range(1, chips):
            cross_copy(j, d).wait_recv()
            total = total + x_recv[j, d - 1].astype(jnp.float32)
        gpk[:, cols(j)] = (total[:, :HD] * factor).astype(jnp.bfloat16)
        gpv[:, cols(j)] = (total[:, HD:] * factor).astype(jnp.bfloat16)
        return carry

    lax.fori_loop(0, KVH, finish, 0)
    ends = [local(gpk, gpk_out.at[0], end_sem.at[0]), local(gpv, gpv_out.at[0], end_sem.at[1])]
    for copy in ends:
        copy.start()

    def drain(j, carry):
        for side in range(2):
            for slot in range(chips):
                direct(side, j, slot).wait_send()
            for d in range(1, chips):
                forward(side, j, d).wait_send()
        sib_copy(j).wait_send()
        for d in range(1, chips):
            cross_copy(j, d).wait_send()
        for kind in range(4):
            out_copy(kind, j).wait()
        return carry

    lax.fori_loop(0, KVH, drain, 0)
    for step in range(1, members):
        stat_copy(step).wait_send()
    tok_copy(0).wait_send()

    @pl.when(node < nodes - 1)
    def _():
        tok_copy(1).wait_send()

    @pl.when(node > 0)
    def _():
        tok_copy(2).wait_send()

    for copy in ends:
        copy.wait()


def place_kernel(*refs):
    count = len(refs) // 3
    sem = refs[-1]
    ins, outs = [], []
    for i in range(count):
        source, out, held = refs[i], refs[count + i], refs[2 * count + i]
        tall = source.shape[-2]
        pieces = 2 if source.shape[-1] > KVH * HD else 1
        for piece in range(pieces):
            span = pl.ds(piece * (tall // pieces), tall // pieces)
            index = (0,) * (len(source.shape) - 2) + (span,)
            spot = len(ins)
            ins.append(pltpu.make_async_copy(source.at[index], held.at[span], sem.at[0, spot]))
            outs.append(pltpu.make_async_copy(held.at[span], out.at[index], sem.at[1, spot]))
    for copy in ins:
        copy.start()
    for copy_in, copy_out in zip(ins, outs):
        copy_in.wait()
        copy_out.start()
    for copy in outs:
        copy.wait()


def body(prompt_k, prompt_v, resp_q, resp_k, resp_v, out_grad, lengths, rewards):
    members = lax.axis_size("member")
    groups = lax.axis_size("group")
    chips = members // 2
    rows = prompt_k.shape[1]
    slots = resp_q.shape[2]
    per_head = resp_q.shape[3] // (KVH * HD)
    keys = members * rows + slots
    width = KVH * HD
    bf, f32 = jnp.bfloat16, jnp.float32
    dma = pltpu.SemaphoreType.DMA
    crossing = max(chips - 1, 1)
    scratch = [
        pltpu.VMEM((keys, width), bf),
        pltpu.VMEM((keys, width), bf),
        pltpu.VMEM((slots, width * per_head), bf),
        pltpu.VMEM((slots, width * per_head), bf),
        pltpu.VMEM((slots, width * per_head), bf),
        pltpu.VMEM((slots, width * per_head), bf),
        pltpu.VMEM((slots, width), f32),
        pltpu.VMEM((slots, width), f32),
        pltpu.VMEM((slots, width), bf),
        pltpu.VMEM((slots, width), bf),
        pltpu.VMEM((rows, width), bf),
        pltpu.VMEM((rows, width), bf),
        pltpu.VMEM((keys, slots * per_head), bf),
        pltpu.VMEM((keys, slots * per_head), bf),
        pltpu.VMEM((keys, slots * per_head), bf),
        pltpu.VMEM((keys, slots * per_head), bf),
        pltpu.VMEM((KVH, members, rows, 2 * HD), f32),
        pltpu.VMEM((KVH, chips, rows, 2 * HD), bf),
        pltpu.VMEM((KVH, chips, rows, 2 * HD), bf),
        pltpu.VMEM((KVH, crossing, rows, 2 * HD), bf),
        pltpu.VMEM((KVH, crossing, rows, 2 * HD), bf),
        pltpu.VMEM((2, 8, HD), f32),
        pltpu.VMEM((members, 2, 8, HD), f32),
        pltpu.VMEM((3, 8, HD), f32),
        pltpu.VMEM((4, 8, HD), f32),
        dma((6,)),
        dma((2, KVH, chips)),
        dma((2, KVH, crossing)),
        dma((2, KVH, members)),
        dma((members,)),
        dma((members,)),
        dma((3,)),
        dma((3,)),
        dma((KVH,)),
        dma((KVH,)),
        dma((KVH, crossing)),
        dma((KVH, crossing)),
        dma((4, KVH)),
        dma((2,)),
    ]
    held = pl.BlockSpec(memory_space=pl.ANY)
    scalar = pl.BlockSpec(memory_space=pltpu.SMEM)
    stored = pl.BlockSpec(memory_space=pltpu.HBM)
    flops = 10 * slots * width * per_head * keys
    moved = sum(2 * a.size * a.dtype.itemsize for a in (resp_q, out_grad, resp_k, resp_v, prompt_k, prompt_v))
    results = pl.pallas_call(
        functools.partial(kernel, groups, members, rows, slots, per_head),
        out_shape=[
            jax.ShapeDtypeStruct(a.shape, bf) for a in (resp_q, resp_q, resp_k, resp_v, prompt_k, prompt_v)
        ],
        in_specs=[scalar, scalar] + [stored] * 6,
        out_specs=[held] * 6,
        scratch_shapes=scratch,
        compiler_params=pltpu.CompilerParams(
            collective_id=0, has_side_effects=True, vmem_limit_bytes=60 * 1024 * 1024),
        cost_estimate=pl.CostEstimate(
            flops=flops, bytes_accessed=moved, transcendentals=slots * KVH * per_head * keys),
        name="shared_prompt_attention",
    )(lengths, rewards, prompt_k, prompt_v, resp_q, resp_k, resp_v, out_grad)
    return pl.pallas_call(
        place_kernel,
        out_shape=[jax.ShapeDtypeStruct(a.shape, bf) for a in results],
        in_specs=[stored] * 6,
        out_specs=[stored] * 6,
        scratch_shapes=[pltpu.VMEM(a.shape[-2:], bf) for a in results] + [dma((2, 8))],
        compiler_params=pltpu.CompilerParams(vmem_limit_bytes=60 * 1024 * 1024),
        cost_estimate=pl.CostEstimate(flops=0, bytes_accessed=moved, transcendentals=0),
        name="place_results",
    )(*results)


def solution(mesh):
    rows = P("group", "member", None)
    wide = P("group", "member", None, None)
    return jax.shard_map(
        body,
        mesh=mesh,
        in_specs=(rows, rows, wide, wide, wide, wide, P("group", "member"), P("group", "member")),
        out_specs=(wide, wide, wide, wide, rows, rows),
        check_vma=False,
    )
```

```python
import functools

import jax
import jax.numpy as jnp
from jax import lax
from jax.experimental import pallas as pl
from jax.experimental.pallas import tpu as pltpu
from jax.sharding import PartitionSpec as P

KVH = 8
HD = 128
LOG2E = 1.4426950408889634
MESH = pl.DeviceIdType.MESH
NT = (((1,), (1,)), ((), ()))
NN = (((1,), (0,)), ((), ()))
TN = (((0,), (0,)), ((), ()))


def dot(a, b, dims):
    return lax.dot_general(a, b, dims, preferred_element_type=jnp.float32)


def kernel(
    groups, members, rows, slots, per_head,
    length_ref, reward_ref, pk_ref, pv_ref, q_ref, rk_ref, rv_ref, og_ref,
    att_out, gq_out, grk_out, grv_out, gpk_out, gpv_out,
    kall, vall, qbuf, obuf, att, gq, grk, grv, grk_low, grv_low, gpk, gpv,
    probs0, probs1, dsc0, dsc1,
    part, sib_send, sib_recv, x_send, x_recv, stat_send, stat, tok_send, tok,
    in_sem, g_send, f_send, g_recv, s_send, s_recv, t_send, t_recv,
    r_send, r_recv, c_send, c_recv, out_sem, end_sem,
):
    chips = members // 2
    prompt = members * rows
    wide = per_head * slots
    score_scale = float(HD) ** (-0.5)
    group = lax.axis_index("group")
    me = lax.axis_index("member")
    chip = lax.div(me, 2)
    core = lax.rem(me, 2)
    sib = chip * 2 + (1 - core)

    def chip_at(d):
        return lax.rem(chip + d, chips)

    def cols(j, width=HD):
        return pl.ds(pl.multiple_of(j * width, width), width)

    def block_rows(owner):
        return pl.ds(pl.multiple_of(owner * rows, rows), rows)

    def local(src, dst, sem):
        return pltpu.make_async_copy(src, dst, sem)

    def remote(src, dst, send, recv, to_group, to_member):
        return pltpu.make_async_remote_copy(
            src_ref=src, dst_ref=dst, send_sem=send, recv_sem=recv,
            device_id=(to_group, to_member), device_id_type=MESH)

    loads = [
        local(pk_ref.at[0], kall.at[block_rows(me)], in_sem.at[0]),
        local(pv_ref.at[0], vall.at[block_rows(me)], in_sem.at[1]),
        local(rk_ref.at[0, 0], kall.at[pl.ds(prompt, slots)], in_sem.at[2]),
        local(rv_ref.at[0, 0], vall.at[pl.ds(prompt, slots)], in_sem.at[3]),
        local(q_ref.at[0, 0], qbuf, in_sem.at[4]),
        local(og_ref.at[0, 0], obuf, in_sem.at[5]),
    ]
    for load in loads:
        load.start()

    barrier = pltpu.get_barrier_semaphore()
    for step in range(1, members):
        pl.semaphore_signal(barrier, inc=1, device_id=(group, lax.rem(me + step, members)), device_id_type=MESH)
    nodes = groups // 2
    node = lax.div(group, 2)
    twin = node * 2 + (1 - lax.rem(group, 2))
    pl.semaphore_signal(barrier, inc=1, device_id=(twin, me), device_id_type=MESH)

    for step in range(1, nodes):
        pl.semaphore_signal(barrier, inc=1, device_id=(lax.rem(group + 2 * step, groups), me), device_id_type=MESH)

    length = length_ref[0, 0]
    stat_send[0] = jnp.full((8, HD), length.astype(jnp.float32))
    stat_send[1] = jnp.full((8, HD), reward_ref[0, 0])
    stat[me] = stat_send[...]
    pl.semaphore_wait(barrier, members + nodes - 1)

    sides = ((pk_ref, kall), (pv_ref, vall))

    def direct(side, j, slot):
        to = sib if slot == 0 else chip_at(slot) * 2 + core
        source, whole = sides[side]
        return remote(source.at[0, :, cols(j)], whole.at[block_rows(me), cols(j)],
                      g_send.at[side, j, slot], g_recv.at[side, j, me], group, to)

    def arrival(side, j, owner):
        place = sides[side][1].at[block_rows(owner), cols(j)]
        return remote(place, place, g_send.at[side, j, 0], g_recv.at[side, j, owner], group, sib)

    def forward(side, j, d):
        owner = chip_at(d) * 2 + core
        place = sides[side][1].at[block_rows(owner), cols(j)]
        return remote(place, place, f_send.at[side, j, d - 1], g_recv.at[side, j, owner], group, sib)

    def stat_copy(step):
        return remote(stat_send, stat.at[me], s_send.at[step - 1], s_recv.at[me], group, lax.rem(me + step, members))

    def twin_copy():
        return remote(tok_send.at[0], tok.at[nodes], t_send.at[0], t_recv.at[nodes], twin, me)

    def tok_copy(step):
        return remote(tok_send.at[1], tok.at[node], t_send.at[step], t_recv.at[node],
                      lax.rem(group + 2 * step, groups), me)

    def far(side, d):
        source, whole = sides[side]
        return remote(source.at[0, :, cols(0)], whole.at[block_rows(me), cols(0)],
                      f_send.at[side, 0, d - 1], g_recv.at[side, 0, me], group, chip_at(d) * 2 + (1 - core))

    def send_head(j, carry):
        for slot in list(range(1, chips)) + [0]:
            for side in range(2):
                direct(side, j, slot).start()
        return carry

    send_head(0, 0)
    for d in range(1, chips):
        for side in range(2):
            far(side, d).start()
    for step in range(1, members):
        stat_copy(step).start()
    lax.fori_loop(1, KVH, send_head, 0)

    def forward_head(j):
        for d in range(1, chips):
            owner = chip_at(d) * 2 + core
            for side in range(2):
                arrival(side, j, owner).wait_recv()
                forward(side, j, d).start()

    def wait_head(j):
        for side in range(2):
            arrival(side, j, sib).wait_recv()
            for d in range(1, chips):
                arrival(side, j, chip_at(d) * 2 + (1 - core)).wait_recv()

    u_pos = lax.broadcasted_iota(jnp.int32, (slots, wide), 0)
    t_pos = lax.rem(lax.broadcasted_iota(jnp.int32, (slots, wide), 1), slots)
    causal = u_pos <= t_pos
    live_lane = lax.rem(lax.broadcasted_iota(jnp.int32, (HD, wide), 1), slots) < length
    live_row = lax.broadcasted_iota(jnp.int32, (slots, per_head * HD), 0) < length

    for load in loads:
        load.wait()

    def mask_head(j, carry):
        g = obuf[:, cols(j, per_head * HD)]
        obuf[:, cols(j, per_head * HD)] = jnp.where(live_row, g, jnp.zeros_like(g))
        return carry

    lax.fori_loop(0, KVH, mask_head, 0)

    def sib_copy(j):
        return remote(sib_send.at[j], sib_recv.at[j], r_send.at[j], r_recv.at[j], group, sib)

    def cross_copy(j, d):
        return remote(x_send.at[j, d - 1], x_recv.at[j, d - 1], c_send.at[j, d - 1], c_recv.at[j, d - 1],
                      group, chip_at(d) * 2 + core)

    def send_part(j):
        for d in range(chips):
            sib_send[j, d] = part[j, chip_at(d) * 2 + (1 - core)].astype(jnp.bfloat16)
        sib_copy(j).start()

    def cross_head(j):
        sib_copy(j).wait_recv()
        for d in range(1, chips):
            own = part[j, chip_at(d) * 2 + core]
            x_send[j, d - 1] = (own + sib_recv[j, d].astype(jnp.float32)).astype(jnp.bfloat16)
            cross_copy(j, d).start()

    def out_copy(kind, j):
        held, out, width = ((att, att_out, per_head * HD), (gq, gq_out, per_head * HD),
                            (grk_low, grk_out, HD), (grv_low, grv_out, HD))[kind]
        return local(held.at[:, cols(j, width)], out.at[0, 0, :, cols(j, width)], out_sem.at[kind, j])

    def stacked(buf, j):
        return jnp.concatenate([buf[:, cols(j * per_head + h)] for h in range(per_head)], axis=0)

    def heads(back, fore, back_bufs, fore_bufs):
        if fore is not None:
            s = dot(kall[:, cols(fore)], stacked(qbuf, fore), NT)
        if back is not None:
            p_back = back_bufs[0][...]
            dv = dot(p_back, stacked(obuf, back), NN) * adv_row
            o_t = dot(vall[:, cols(back)], p_back, TN)
        if fore is not None:
            s = jnp.concatenate([s[:prompt], jnp.where(causal, s[prompt:], -1e30)], axis=0)
            top = jnp.max(s, axis=0, keepdims=True)
            e = jnp.exp2((s - top) * (score_scale * LOG2E))
            p = e * (1.0 / jnp.sum(e, axis=0, keepdims=True))
            fore_bufs[0][...] = p.astype(jnp.bfloat16)
            dp = dot(vall[:, cols(fore)], stacked(obuf, fore), NT)
        if back is not None:
            ds_back = back_bufs[1][...]
            dk = dot(ds_back, stacked(qbuf, back), NN) * (adv_row * score_scale)
            dq_t = dot(kall[:, cols(back)], ds_back, TN) * (adv_one * score_scale)
        if fore is not None:
            delta = jnp.sum(p * dp, axis=0, keepdims=True)
            fore_bufs[1][...] = (p * (dp - delta)).astype(jnp.bfloat16)
        if back is not None:
            part[back, :, :, :HD] = dk[:prompt].reshape(members, rows, HD)
            part[back, :, :, HD:] = dv[:prompt].reshape(members, rows, HD)
            if fore is None:
                send_part(back)
            grk[:, cols(back)] = dk[prompt:]
            grv[:, cols(back)] = dv[prompt:]
            o_t = jnp.where(live_lane, o_t, 0.0).astype(jnp.bfloat16)
            dq_t = dq_t.astype(jnp.bfloat16)
            for h in range(per_head):
                att[:, cols(back * per_head + h)] = o_t[:, h * slots:(h + 1) * slots].T
                gq[:, cols(back * per_head + h)] = dq_t[:, h * slots:(h + 1) * slots].T
            if fore is not None:
                send_part(back)
            out_copy(0, back).start()

    bufs = ((probs0, dsc0), (probs1, dsc1))
    wait_head(0)
    for side in range(2):
        for d in range(1, chips):
            arrival(side, 0, chip_at(d) * 2 + core).wait_recv()
    forward_head(1)
    heads(None, 0, None, bufs[0])
    for step in range(1, members):
        owner = lax.rem(me + step, members)
        remote(stat_send, stat.at[owner], s_send.at[0], s_recv.at[owner], group, owner).wait_recv()
    tok_send[0] = functools.reduce(jnp.add, [stat[i, 0] for i in range(members)])
    twin_copy().start()
    reward_total = functools.reduce(jnp.add, [stat[i, 1] for i in range(members)])
    advantage = stat_send[1] - reward_total / members
    adv_row = advantage[0:1]
    adv_one = adv_row[:, 0:1]

    def pair(i, carry):
        j = 2 * i
        forward_head(j + 2)
        wait_head(j + 1)
        heads(j, j + 1, bufs[0], bufs[1])

        @pl.when(i > 0)
        def _():
            cross_head(j - 1)

        @pl.when(i == 0)
        def _():
            twin_copy().wait_recv()
            tok_send[1] = tok_send[0] + tok[nodes]
            tok[node] = tok_send[1]
            for step in range(1, nodes):
                tok_copy(step).start()

        forward_head(j + 3)
        wait_head(j + 2)
        heads(j + 1, j + 2, bufs[1], bufs[0])
        cross_head(j)
        return carry

    lax.fori_loop(0, KVH // 2 - 1, pair, 0)
    wait_head(KVH - 1)
    heads(KVH - 2, KVH - 1, bufs[0], bufs[1])
    cross_head(KVH - 3)
    heads(KVH - 1, None, bufs[1], None)
    cross_head(KVH - 2)
    for step in range(1, nodes):
        owner = lax.rem(node + step, nodes)
        remote(tok_send.at[1], tok.at[owner], t_send.at[0], t_recv.at[owner], twin, me).wait_recv()
    tokens = functools.reduce(jnp.add, [tok[i] for i in range(nodes)])
    factor = (float(slots * groups * members) / tokens)[0:1]
    factor_one = factor[:, 0:1]

    def scale_head(j, carry):
        span = cols(j, per_head * HD)
        gq[:, span] = (gq[:, span].astype(jnp.float32) * factor_one).astype(jnp.bfloat16)
        grk_low[:, cols(j)] = (grk[:, cols(j)] * factor).astype(jnp.bfloat16)
        grv_low[:, cols(j)] = (grv[:, cols(j)] * factor).astype(jnp.bfloat16)
        for kind in range(1, 4):
            out_copy(kind, j).start()
        return carry

    lax.fori_loop(0, KVH // 2, scale_head, 0)
    cross_head(KVH - 1)
    lax.fori_loop(KVH // 2, KVH, scale_head, 0)

    def finish(j, carry):
        total = part[j, me] + sib_recv[j, 0].astype(jnp.float32)
        for d in range(1, chips):
            cross_copy(j, d).wait_recv()
            total = total + x_recv[j, d - 1].astype(jnp.float32)
        gpk[:, cols(j)] = (total[:, :HD] * factor).astype(jnp.bfloat16)
        gpv[:, cols(j)] = (total[:, HD:] * factor).astype(jnp.bfloat16)
        return carry

    lax.fori_loop(0, KVH, finish, 0)
    ends = [local(gpk, gpk_out.at[0], end_sem.at[0]), local(gpv, gpv_out.at[0], end_sem.at[1])]
    for copy in ends:
        copy.start()

    def drain(j, carry):
        for side in range(2):
            for slot in range(chips):
                direct(side, j, slot).wait_send()
            for d in range(1, chips):
                forward(side, j, d).wait_send()
        sib_copy(j).wait_send()
        for d in range(1, chips):
            cross_copy(j, d).wait_send()
        for kind in range(4):
            out_copy(kind, j).wait()
        return carry

    lax.fori_loop(0, KVH, drain, 0)
    for step in range(1, members):
        stat_copy(step).wait_send()
    twin_copy().wait_send()
    for step in range(1, nodes):
        tok_copy(step).wait_send()
    for copy in ends:
        copy.wait()


def place_kernel(*refs):
    count = len(refs) // 3
    sem = refs[-1]
    ins, outs = [], []
    for i in range(count):
        source, out, held = refs[i], refs[count + i], refs[2 * count + i]
        tall = source.shape[-2]
        pieces = 2 if source.shape[-1] > KVH * HD else 1
        for piece in range(pieces):
            span = pl.ds(piece * (tall // pieces), tall // pieces)
            index = (0,) * (len(source.shape) - 2) + (span,)
            spot = len(ins)
            ins.append(pltpu.make_async_copy(source.at[index], held.at[span], sem.at[0, spot]))
            outs.append(pltpu.make_async_copy(held.at[span], out.at[index], sem.at[1, spot]))
    for copy in ins:
        copy.start()
    for copy_in, copy_out in zip(ins, outs):
        copy_in.wait()
        copy_out.start()
    for copy in outs:
        copy.wait()


def body(prompt_k, prompt_v, resp_q, resp_k, resp_v, out_grad, lengths, rewards):
    members = lax.axis_size("member")
    groups = lax.axis_size("group")
    chips = members // 2
    rows = prompt_k.shape[1]
    slots = resp_q.shape[2]
    per_head = resp_q.shape[3] // (KVH * HD)
    keys = members * rows + slots
    width = KVH * HD
    bf, f32 = jnp.bfloat16, jnp.float32
    dma = pltpu.SemaphoreType.DMA
    crossing = max(chips - 1, 1)
    scratch = [
        pltpu.VMEM((keys, width), bf),
        pltpu.VMEM((keys, width), bf),
        pltpu.VMEM((slots, width * per_head), bf),
        pltpu.VMEM((slots, width * per_head), bf),
        pltpu.VMEM((slots, width * per_head), bf),
        pltpu.VMEM((slots, width * per_head), bf),
        pltpu.VMEM((slots, width), f32),
        pltpu.VMEM((slots, width), f32),
        pltpu.VMEM((slots, width), bf),
        pltpu.VMEM((slots, width), bf),
        pltpu.VMEM((rows, width), bf),
        pltpu.VMEM((rows, width), bf),
        pltpu.VMEM((keys, slots * per_head), bf),
        pltpu.VMEM((keys, slots * per_head), bf),
        pltpu.VMEM((keys, slots * per_head), bf),
        pltpu.VMEM((keys, slots * per_head), bf),
        pltpu.VMEM((KVH, members, rows, 2 * HD), f32),
        pltpu.VMEM((KVH, chips, rows, 2 * HD), bf),
        pltpu.VMEM((KVH, chips, rows, 2 * HD), bf),
        pltpu.VMEM((KVH, crossing, rows, 2 * HD), bf),
        pltpu.VMEM((KVH, crossing, rows, 2 * HD), bf),
        pltpu.VMEM((2, 8, HD), f32),
        pltpu.VMEM((members, 2, 8, HD), f32),
        pltpu.VMEM((2, 8, HD), f32),
        pltpu.VMEM((groups // 2 + 1, 8, HD), f32),
        dma((6,)),
        dma((2, KVH, chips)),
        dma((2, KVH, crossing)),
        dma((2, KVH, members)),
        dma((members,)),
        dma((members,)),
        dma((groups // 2,)),
        dma((groups // 2 + 1,)),
        dma((KVH,)),
        dma((KVH,)),
        dma((KVH, crossing)),
        dma((KVH, crossing)),
        dma((4, KVH)),
        dma((2,)),
    ]
    held = pl.BlockSpec(memory_space=pl.ANY)
    scalar = pl.BlockSpec(memory_space=pltpu.SMEM)
    stored = pl.BlockSpec(memory_space=pltpu.HBM)
    flops = 10 * slots * width * per_head * keys
    moved = sum(2 * a.size * a.dtype.itemsize for a in (resp_q, out_grad, resp_k, resp_v, prompt_k, prompt_v))
    results = pl.pallas_call(
        functools.partial(kernel, groups, members, rows, slots, per_head),
        out_shape=[
            jax.ShapeDtypeStruct(a.shape, bf) for a in (resp_q, resp_q, resp_k, resp_v, prompt_k, prompt_v)
        ],
        in_specs=[scalar, scalar] + [stored] * 6,
        out_specs=[held] * 6,
        scratch_shapes=scratch,
        compiler_params=pltpu.CompilerParams(
            collective_id=0, has_side_effects=True, vmem_limit_bytes=60 * 1024 * 1024),
        cost_estimate=pl.CostEstimate(
            flops=flops, bytes_accessed=moved, transcendentals=slots * KVH * per_head * keys),
        name="shared_prompt_attention",
    )(lengths, rewards, prompt_k, prompt_v, resp_q, resp_k, resp_v, out_grad)
    return pl.pallas_call(
        place_kernel,
        out_shape=[jax.ShapeDtypeStruct(a.shape, bf) for a in results],
        in_specs=[stored] * 6,
        out_specs=[stored] * 6,
        scratch_shapes=[pltpu.VMEM(a.shape[-2:], bf) for a in results] + [dma((2, 8))],
        compiler_params=pltpu.CompilerParams(vmem_limit_bytes=60 * 1024 * 1024),
        cost_estimate=pl.CostEstimate(flops=0, bytes_accessed=moved, transcendentals=0),
        name="place_results",
    )(*results)


def solution(mesh):
    rows = P("group", "member", None)
    wide = P("group", "member", None, None)
    return jax.shard_map(
        body,
        mesh=mesh,
        in_specs=(rows, rows, wide, wide, wide, wide, P("group", "member"), P("group", "member")),
        out_specs=(wide, wide, wide, wide, rows, rows),
        check_vma=False,
    )
```

```python
import functools

import jax
import jax.numpy as jnp
from jax import lax
from jax.experimental import pallas as pl
from jax.experimental.pallas import tpu as pltpu
from jax.sharding import PartitionSpec as P

KVH = 8
HD = 128
LOG2E = 1.4426950408889634
MESH = pl.DeviceIdType.MESH
NT = (((1,), (1,)), ((), ()))
NN = (((1,), (0,)), ((), ()))
TN = (((0,), (0,)), ((), ()))


def dot(a, b, dims):
    return lax.dot_general(a, b, dims, preferred_element_type=jnp.float32)


def kernel(
    groups, members, rows, slots, per_head,
    length_ref, reward_ref, pk_ref, pv_ref, q_ref, rk_ref, rv_ref, og_ref,
    att_out, gq_out, grk_out, grv_out, gpk_out, gpv_out,
    kall, vall, qbuf, obuf, att, gq, grk, grv, grk_low, grv_low, gpk, gpv,
    probs0, probs1, dsc0, dsc1,
    part, sib_send, sib_recv, x_send, x_recv, stat_send, stat, tok_send, tok,
    in_sem, g_send, f_send, g_recv, s_send, s_recv, t_send, t_recv,
    r_send, r_recv, c_send, c_recv, out_sem, end_sem,
):
    chips = members // 2
    prompt = members * rows
    wide = per_head * slots
    score_scale = float(HD) ** (-0.5)
    group = lax.axis_index("group")
    me = lax.axis_index("member")
    chip = lax.div(me, 2)
    core = lax.rem(me, 2)
    sib = chip * 2 + (1 - core)

    def chip_at(d):
        return lax.rem(chip + d, chips)

    def cols(j, width=HD):
        return pl.ds(pl.multiple_of(j * width, width), width)

    def block_rows(owner):
        return pl.ds(pl.multiple_of(owner * rows, rows), rows)

    def local(src, dst, sem):
        return pltpu.make_async_copy(src, dst, sem)

    def remote(src, dst, send, recv, to_group, to_member):
        return pltpu.make_async_remote_copy(
            src_ref=src, dst_ref=dst, send_sem=send, recv_sem=recv,
            device_id=(to_group, to_member), device_id_type=MESH)

    loads = [
        local(pk_ref.at[0], kall.at[block_rows(me)], in_sem.at[0]),
        local(pv_ref.at[0], vall.at[block_rows(me)], in_sem.at[1]),
        local(rk_ref.at[0, 0], kall.at[pl.ds(prompt, slots)], in_sem.at[2]),
        local(rv_ref.at[0, 0], vall.at[pl.ds(prompt, slots)], in_sem.at[3]),
        local(q_ref.at[0, 0], qbuf, in_sem.at[4]),
        local(og_ref.at[0, 0], obuf, in_sem.at[5]),
    ]
    for load in loads:
        load.start()

    barrier = pltpu.get_barrier_semaphore()
    for step in range(1, members):
        pl.semaphore_signal(barrier, inc=1, device_id=(group, lax.rem(me + step, members)), device_id_type=MESH)
    nodes = groups // 2
    node = lax.div(group, 2)
    twin = node * 2 + (1 - lax.rem(group, 2))
    pl.semaphore_signal(barrier, inc=1, device_id=(twin, me), device_id_type=MESH)

    @pl.when(node > 0)
    def _():
        pl.semaphore_signal(barrier, inc=1, device_id=(group - 2, me), device_id_type=MESH)

    @pl.when(node < nodes - 1)
    def _():
        pl.semaphore_signal(barrier, inc=1, device_id=(group + 2, me), device_id_type=MESH)


    length = length_ref[0, 0]
    stat_send[0] = jnp.full((8, HD), length.astype(jnp.float32))
    stat_send[1] = jnp.full((8, HD), reward_ref[0, 0])
    stat[me] = stat_send[...]
    ends = (node == 0).astype(jnp.int32) + (node == nodes - 1).astype(jnp.int32)
    pl.semaphore_wait(barrier, members + 2 - ends)

    sides = ((pk_ref, kall), (pv_ref, vall))

    def direct(side, j, slot):
        to = sib if slot == 0 else chip_at(slot) * 2 + core
        source, whole = sides[side]
        return remote(source.at[0, :, cols(j)], whole.at[block_rows(me), cols(j)],
                      g_send.at[side, j, slot], g_recv.at[side, j, me], group, to)

    def arrival(side, j, owner):
        place = sides[side][1].at[block_rows(owner), cols(j)]
        return remote(place, place, g_send.at[side, j, 0], g_recv.at[side, j, owner], group, sib)

    def forward(side, j, d):
        owner = chip_at(d) * 2 + core
        place = sides[side][1].at[block_rows(owner), cols(j)]
        return remote(place, place, f_send.at[side, j, d - 1], g_recv.at[side, j, owner], group, sib)

    def stat_copy(step):
        return remote(stat_send, stat.at[me], s_send.at[step - 1], s_recv.at[me], group, lax.rem(me + step, members))

    def tok_copy(kind):
        to = (twin, group + 2, group - 2)[kind]
        return remote(tok_send.at[kind], tok.at[kind], t_send.at[kind], t_recv.at[kind], to, me)

    def relay(slot):
        @pl.when(2 * node == slot)
        def _():
            @pl.when(node > 0)
            def _():
                tok_copy(1).wait_recv()
                tok_send[1] = tok[1] + tok[3]

            @pl.when(node == 0)
            def _():
                tok_send[1] = tok[3]

            @pl.when(node < nodes - 1)
            def _():
                tok_copy(1).start()

        @pl.when(2 * (nodes - 1 - node) == slot)
        def _():
            @pl.when(node < nodes - 1)
            def _():
                tok_copy(2).wait_recv()
                tok_send[2] = tok[2] + tok[3]

            @pl.when(node == nodes - 1)
            def _():
                tok_send[2] = tok[3]

            @pl.when(node > 0)
            def _():
                tok_copy(2).start()

    def far(side, d):
        source, whole = sides[side]
        return remote(source.at[0, :, cols(0)], whole.at[block_rows(me), cols(0)],
                      f_send.at[side, 0, d - 1], g_recv.at[side, 0, me], group, chip_at(d) * 2 + (1 - core))

    def send_head(j, carry):
        for slot in list(range(1, chips)) + [0]:
            for side in range(2):
                direct(side, j, slot).start()
        return carry

    send_head(0, 0)
    for d in range(1, chips):
        for side in range(2):
            far(side, d).start()
    for step in range(1, members):
        stat_copy(step).start()
    lax.fori_loop(1, KVH, send_head, 0)

    def forward_head(j):
        for d in range(1, chips):
            owner = chip_at(d) * 2 + core
            for side in range(2):
                arrival(side, j, owner).wait_recv()
                forward(side, j, d).start()

    def wait_head(j):
        for side in range(2):
            arrival(side, j, sib).wait_recv()
            for d in range(1, chips):
                arrival(side, j, chip_at(d) * 2 + (1 - core)).wait_recv()

    u_pos = lax.broadcasted_iota(jnp.int32, (slots, wide), 0)
    t_pos = lax.rem(lax.broadcasted_iota(jnp.int32, (slots, wide), 1), slots)
    causal = u_pos <= t_pos
    live_lane = lax.rem(lax.broadcasted_iota(jnp.int32, (HD, wide), 1), slots) < length
    live_row = lax.broadcasted_iota(jnp.int32, (slots, per_head * HD), 0) < length

    for load in loads:
        load.wait()

    def mask_head(j, carry):
        g = obuf[:, cols(j, per_head * HD)]
        obuf[:, cols(j, per_head * HD)] = jnp.where(live_row, g, jnp.zeros_like(g))
        return carry

    lax.fori_loop(0, KVH, mask_head, 0)

    def sib_copy(j):
        return remote(sib_send.at[j], sib_recv.at[j], r_send.at[j], r_recv.at[j], group, sib)

    def cross_copy(j, d):
        return remote(x_send.at[j, d - 1], x_recv.at[j, d - 1], c_send.at[j, d - 1], c_recv.at[j, d - 1],
                      group, chip_at(d) * 2 + core)

    def send_part(j):
        for d in range(chips):
            sib_send[j, d] = part[j, chip_at(d) * 2 + (1 - core)].astype(jnp.bfloat16)
        sib_copy(j).start()

    def cross_head(j):
        sib_copy(j).wait_recv()
        for d in range(1, chips):
            own = part[j, chip_at(d) * 2 + core]
            x_send[j, d - 1] = (own + sib_recv[j, d].astype(jnp.float32)).astype(jnp.bfloat16)
            cross_copy(j, d).start()

    def out_copy(kind, j):
        held, out, width = ((att, att_out, per_head * HD), (gq, gq_out, per_head * HD),
                            (grk_low, grk_out, HD), (grv_low, grv_out, HD))[kind]
        return local(held.at[:, cols(j, width)], out.at[0, 0, :, cols(j, width)], out_sem.at[kind, j])

    def stacked(buf, j):
        return jnp.concatenate([buf[:, cols(j * per_head + h)] for h in range(per_head)], axis=0)

    def heads(back, fore, back_bufs, fore_bufs):
        if fore is not None:
            s = dot(kall[:, cols(fore)], stacked(qbuf, fore), NT)
        if back is not None:
            p_back = back_bufs[0][...]
            dv = dot(p_back, stacked(obuf, back), NN) * adv_row
            o_t = dot(vall[:, cols(back)], p_back, TN)
        if fore is not None:
            s = jnp.concatenate([s[:prompt], jnp.where(causal, s[prompt:], -1e30)], axis=0)
            top = jnp.max(s, axis=0, keepdims=True)
            e = jnp.exp2((s - top) * (score_scale * LOG2E))
            p = e * (1.0 / jnp.sum(e, axis=0, keepdims=True))
            fore_bufs[0][...] = p.astype(jnp.bfloat16)
            dp = dot(vall[:, cols(fore)], stacked(obuf, fore), NT)
        if back is not None:
            ds_back = back_bufs[1][...]
            dk = dot(ds_back, stacked(qbuf, back), NN) * (adv_row * score_scale)
            dq_t = dot(kall[:, cols(back)], ds_back, TN) * (adv_one * score_scale)
        if fore is not None:
            delta = jnp.sum(p * dp, axis=0, keepdims=True)
            fore_bufs[1][...] = (p * (dp - delta)).astype(jnp.bfloat16)
        if back is not None:
            part[back, :, :, :HD] = dk[:prompt].reshape(members, rows, HD)
            part[back, :, :, HD:] = dv[:prompt].reshape(members, rows, HD)
            if fore is None:
                send_part(back)
            grk[:, cols(back)] = dk[prompt:]
            grv[:, cols(back)] = dv[prompt:]
            o_t = jnp.where(live_lane, o_t, 0.0).astype(jnp.bfloat16)
            dq_t = dq_t.astype(jnp.bfloat16)
            for h in range(per_head):
                att[:, cols(back * per_head + h)] = o_t[:, h * slots:(h + 1) * slots].T
                gq[:, cols(back * per_head + h)] = dq_t[:, h * slots:(h + 1) * slots].T
            if fore is not None:
                send_part(back)
            out_copy(0, back).start()

    bufs = ((probs0, dsc0), (probs1, dsc1))
    wait_head(0)
    for side in range(2):
        for d in range(1, chips):
            arrival(side, 0, chip_at(d) * 2 + core).wait_recv()
    forward_head(1)
    heads(None, 0, None, bufs[0])
    for step in range(1, members):
        owner = lax.rem(me + step, members)
        remote(stat_send, stat.at[owner], s_send.at[0], s_recv.at[owner], group, owner).wait_recv()
    tok_send[0] = functools.reduce(jnp.add, [stat[i, 0] for i in range(members)])
    tok_copy(0).start()
    reward_total = functools.reduce(jnp.add, [stat[i, 1] for i in range(members)])
    advantage = stat_send[1] - reward_total / members
    adv_row = advantage[0:1]
    adv_one = adv_row[:, 0:1]

    def pair(i, carry):
        j = 2 * i
        forward_head(j + 2)
        wait_head(j + 1)
        heads(j, j + 1, bufs[0], bufs[1])

        @pl.when(i > 0)
        def _():
            cross_head(j - 1)

        @pl.when(i == 0)
        def _():
            tok_copy(0).wait_recv()
            tok[3] = tok_send[0] + tok[0]

        relay(j)
        forward_head(j + 3)
        wait_head(j + 2)
        heads(j + 1, j + 2, bufs[1], bufs[0])
        cross_head(j)
        relay(j + 1)
        return carry

    lax.fori_loop(0, KVH // 2 - 1, pair, 0)
    wait_head(KVH - 1)
    heads(KVH - 2, KVH - 1, bufs[0], bufs[1])
    cross_head(KVH - 3)
    heads(KVH - 1, None, bufs[1], None)
    cross_head(KVH - 2)
    cross_head(KVH - 1)
    for slot in range(KVH - 2, 2 * nodes - 1):
        relay(slot)
    tokens = tok[3]
    before = jnp.where(node > 0, tok_send[1] - tok[3], jnp.zeros_like(tokens))
    after = jnp.where(node < nodes - 1, tok_send[2] - tok[3], jnp.zeros_like(tokens))
    tokens = tokens + before + after
    factor = (float(slots * groups * members) / tokens)[0:1]
    factor_one = factor[:, 0:1]

    def scale_head(j, carry):
        span = cols(j, per_head * HD)
        gq[:, span] = (gq[:, span].astype(jnp.float32) * factor_one).astype(jnp.bfloat16)
        grk_low[:, cols(j)] = (grk[:, cols(j)] * factor).astype(jnp.bfloat16)
        grv_low[:, cols(j)] = (grv[:, cols(j)] * factor).astype(jnp.bfloat16)
        for kind in range(1, 4):
            out_copy(kind, j).start()
        return carry

    lax.fori_loop(0, KVH, scale_head, 0)

    def finish(j, carry):
        total = part[j, me] + sib_recv[j, 0].astype(jnp.float32)
        for d in range(1, chips):
            cross_copy(j, d).wait_recv()
            total = total + x_recv[j, d - 1].astype(jnp.float32)
        gpk[:, cols(j)] = (total[:, :HD] * factor).astype(jnp.bfloat16)
        gpv[:, cols(j)] = (total[:, HD:] * factor).astype(jnp.bfloat16)
        return carry

    lax.fori_loop(0, KVH, finish, 0)
    ends = [local(gpk, gpk_out.at[0], end_sem.at[0]), local(gpv, gpv_out.at[0], end_sem.at[1])]
    for copy in ends:
        copy.start()

    def drain(j, carry):
        for side in range(2):
            for slot in range(chips):
                direct(side, j, slot).wait_send()
            for d in range(1, chips):
                forward(side, j, d).wait_send()
        sib_copy(j).wait_send()
        for d in range(1, chips):
            cross_copy(j, d).wait_send()
        for kind in range(4):
            out_copy(kind, j).wait()
        return carry

    lax.fori_loop(0, KVH, drain, 0)
    for step in range(1, members):
        stat_copy(step).wait_send()
    tok_copy(0).wait_send()

    @pl.when(node < nodes - 1)
    def _():
        tok_copy(1).wait_send()

    @pl.when(node > 0)
    def _():
        tok_copy(2).wait_send()

    for copy in ends:
        copy.wait()


def place_kernel(*refs):
    count = len(refs) // 3
    sem = refs[-1]
    ins, outs = [], []
    for i in range(count):
        source, out, held = refs[i], refs[count + i], refs[2 * count + i]
        tall = source.shape[-2]
        pieces = 2 if source.shape[-1] > KVH * HD else 1
        for piece in range(pieces):
            span = pl.ds(piece * (tall // pieces), tall // pieces)
            index = (0,) * (len(source.shape) - 2) + (span,)
            spot = len(ins)
            ins.append(pltpu.make_async_copy(source.at[index], held.at[span], sem.at[0, spot]))
            outs.append(pltpu.make_async_copy(held.at[span], out.at[index], sem.at[1, spot]))
    for copy in ins:
        copy.start()
    for copy_in, copy_out in zip(ins, outs):
        copy_in.wait()
        copy_out.start()
    for copy in outs:
        copy.wait()


def body(prompt_k, prompt_v, resp_q, resp_k, resp_v, out_grad, lengths, rewards):
    members = lax.axis_size("member")
    groups = lax.axis_size("group")
    chips = members // 2
    rows = prompt_k.shape[1]
    slots = resp_q.shape[2]
    per_head = resp_q.shape[3] // (KVH * HD)
    keys = members * rows + slots
    width = KVH * HD
    bf, f32 = jnp.bfloat16, jnp.float32
    dma = pltpu.SemaphoreType.DMA
    crossing = max(chips - 1, 1)
    scratch = [
        pltpu.VMEM((keys, width), bf),
        pltpu.VMEM((keys, width), bf),
        pltpu.VMEM((slots, width * per_head), bf),
        pltpu.VMEM((slots, width * per_head), bf),
        pltpu.VMEM((slots, width * per_head), bf),
        pltpu.VMEM((slots, width * per_head), bf),
        pltpu.VMEM((slots, width), f32),
        pltpu.VMEM((slots, width), f32),
        pltpu.VMEM((slots, width), bf),
        pltpu.VMEM((slots, width), bf),
        pltpu.VMEM((rows, width), bf),
        pltpu.VMEM((rows, width), bf),
        pltpu.VMEM((keys, slots * per_head), bf),
        pltpu.VMEM((keys, slots * per_head), bf),
        pltpu.VMEM((keys, slots * per_head), bf),
        pltpu.VMEM((keys, slots * per_head), bf),
        pltpu.VMEM((KVH, members, rows, 2 * HD), f32),
        pltpu.VMEM((KVH, chips, rows, 2 * HD), bf),
        pltpu.VMEM((KVH, chips, rows, 2 * HD), bf),
        pltpu.VMEM((KVH, crossing, rows, 2 * HD), bf),
        pltpu.VMEM((KVH, crossing, rows, 2 * HD), bf),
        pltpu.VMEM((2, 8, HD), f32),
        pltpu.VMEM((members, 2, 8, HD), f32),
        pltpu.VMEM((3, 8, HD), f32),
        pltpu.VMEM((4, 8, HD), f32),
        dma((6,)),
        dma((2, KVH, chips)),
        dma((2, KVH, crossing)),
        dma((2, KVH, members)),
        dma((members,)),
        dma((members,)),
        dma((3,)),
        dma((3,)),
        dma((KVH,)),
        dma((KVH,)),
        dma((KVH, crossing)),
        dma((KVH, crossing)),
        dma((4, KVH)),
        dma((2,)),
    ]
    held = pl.BlockSpec(memory_space=pl.ANY)
    scalar = pl.BlockSpec(memory_space=pltpu.SMEM)
    stored = pl.BlockSpec(memory_space=pltpu.HBM)
    flops = 10 * slots * width * per_head * keys
    moved = sum(2 * a.size * a.dtype.itemsize for a in (resp_q, out_grad, resp_k, resp_v, prompt_k, prompt_v))
    results = pl.pallas_call(
        functools.partial(kernel, groups, members, rows, slots, per_head),
        out_shape=[
            jax.ShapeDtypeStruct(a.shape, bf) for a in (resp_q, resp_q, resp_k, resp_v, prompt_k, prompt_v)
        ],
        in_specs=[scalar, scalar] + [stored] * 6,
        out_specs=[held] * 6,
        scratch_shapes=scratch,
        compiler_params=pltpu.CompilerParams(
            collective_id=0, has_side_effects=True, vmem_limit_bytes=60 * 1024 * 1024),
        cost_estimate=pl.CostEstimate(
            flops=flops, bytes_accessed=moved, transcendentals=slots * KVH * per_head * keys),
        name="shared_prompt_attention",
    )(lengths, rewards, prompt_k, prompt_v, resp_q, resp_k, resp_v, out_grad)
    return pl.pallas_call(
        place_kernel,
        out_shape=[jax.ShapeDtypeStruct(a.shape, bf) for a in results],
        in_specs=[stored] * 6,
        out_specs=[stored] * 6,
        scratch_shapes=[pltpu.VMEM(a.shape[-2:], bf) for a in results] + [dma((2, 8))],
        compiler_params=pltpu.CompilerParams(vmem_limit_bytes=60 * 1024 * 1024),
        cost_estimate=pl.CostEstimate(flops=0, bytes_accessed=moved, transcendentals=0),
        name="place_results",
    )(*results)


def solution(mesh):
    rows = P("group", "member", None)
    wide = P("group", "member", None, None)
    return jax.shard_map(
        body,
        mesh=mesh,
        in_specs=(rows, rows, wide, wide, wide, wide, P("group", "member"), P("group", "member")),
        out_specs=(wide, wide, wide, wide, rows, rows),
        check_vma=False,
    )
```
